256 devices in a mesh: dp: 2 (over z_hi), ctx: 8 (over z_lo, core), vocab: 16 (over x, y).
Axes of the slice: x: 4, y: 4, z: 8 (z_hi: 2, z_lo: 4; z = z_hi * 4 + z_lo), core: 2. Of those that a mesh axis runs over, the one named last changes fastest.
Arguments:
- hidden: bfloat16 [1024, 4096], P(('dp', 'ctx')), may hold values from -32 to 32
- head_weight: bfloat16 [4096, 76032], P(None, ('ctx', 'vocab')), may hold values from -2 to 2
- targets: int32 [1024], P('dp'), may hold values from 0 to 76031
- segment_ids: int32 [1024], P('dp'), may hold values from 0 to 63, as said below
- lengths: int32 [64], replicated, may hold values from 8 to 24, as said below
- loss_mask: int32 [1024], P('dp'), may hold values 0 or 1
- advantages: float32 [64], replicated, may hold values from -4 to 4
- ref_logprobs: float32 [1024], P('dp'), may hold values from -40 to -2
Outputs:
- grad_hidden: bfloat16 [1024, 4096], P(('dp', 'ctx', 'vocab'))
- grad_head: bfloat16 [4096, 76032], P(None, ('ctx', 'vocab'))
The draws below stay inside these ranges and needn't reach their ends.
Inputs may be any that keep to these rules, and one draw needn't show every extreme that they name: `segment_ids`: each sequence's tokens are contiguous; the tokens b * 64 to (b + 1) * 64 - 1 carry ids b * 4 to (b + 1) * 4 - 1, never falling, each id used. lengths[s] is the number of tokens whose segment id is s.
All inputs are finite; a program needn't handle non-finite values. No bound on the sum of `loss_mask` on one device may be relied on, other than what follows from the above.
Results may differ from the reference program's by a relative error of at most 0.012.
Values may be sent and summed in bfloat16 or wider, within the bound.
No kernel may reach another device: no remote copies, remote signals or barrier semaphores. Data moves between devices by JAX's collectives and lax.ppermute only.
A program may use at most 128 MiB of HBM per device.

```python
import math
import jax
import jax.numpy as jnp
import numpy as np
from jax import lax

D = 4096
V_DEV = 594
TOK_DEV = 64
SEQ_DEV = 4
LOSS_SCALE = 1024
V = 76032
TOK_GRP = 512
TOKENS = 1024
N_SEQ = 64
N_DP = 2
N_CTX = 8
N_VOCAB = 16


def plan_lengths(key):
    block_total = N_DP * N_CTX
    base_length = TOK_DEV // (2 * SEQ_DEV)
    spare_tokens = TOK_DEV - SEQ_DEV * base_length
    big_extra = (spare_tokens + 1) // 2
    rest_tokens = spare_tokens - big_extra
    cut_points = jnp.sort(jax.random.randint(jax.random.fold_in(key, 11), (block_total, SEQ_DEV - 2), 0, rest_tokens + 1), axis=1)
    boundaries = jnp.concatenate([jnp.zeros((block_total, 1), jnp.int32), cut_points.astype(jnp.int32), jnp.full((block_total, 1), rest_tokens, jnp.int32)], axis=1)
    others = base_length + boundaries[:, 1:] - boundaries[:, :-1]
    big_place = jax.random.randint(jax.random.fold_in(key, 13), (block_total, 1), 0, SEQ_DEV)
    slot = jnp.arange(SEQ_DEV, dtype=jnp.int32)[None, :]
    other_index = jnp.clip(slot - (slot > big_place).astype(jnp.int32), 0, SEQ_DEV - 2)
    picked = jnp.take_along_axis(others, other_index, axis=1)
    return jnp.where(slot == big_place, base_length + big_extra, picked).astype(jnp.int32)


def draw_lengths(key, part):
    return plan_lengths(key).reshape(-1).astype(jnp.int32)


def draw_segment_ids(key, part):
    seq_sizes = plan_lengths(key)
    seq_ends = jnp.cumsum(seq_sizes, axis=1)
    position = jnp.arange(TOK_DEV, dtype=jnp.int32)
    local_index = jnp.sum((position[None, :, None] >= seq_ends[:, None, :-1]).astype(jnp.int32), axis=2)
    offsets = SEQ_DEV * jnp.arange(N_DP * N_CTX, dtype=jnp.int32)
    return (local_index + offsets[:, None]).reshape(-1).astype(jnp.int32)


def draw_hidden(key, part):
    noise = jax.random.truncated_normal(jax.random.fold_in(key, 1), -5.0, 5.0, (TOKENS, D), jnp.float32)
    row_scales = jnp.exp(jax.random.uniform(jax.random.fold_in(key, 5), (TOKENS,), jnp.float32, jnp.log(0.3), jnp.log(3.0)))
    matrix = row_scales[:, None] * noise
    return jnp.clip(matrix, -32.0, 32.0).astype(jnp.bfloat16)


def draw_head_weight(key, part):
    noise = jax.random.truncated_normal(jax.random.fold_in(key, 2), -5.0, 5.0, (D, V), jnp.float32) / jnp.sqrt(float(D))
    position = jnp.arange(V, dtype=jnp.float32) / V
    spread = jnp.exp(jax.random.uniform(jax.random.fold_in(key, 4), (V,), jnp.float32, 0.0, jnp.log(10.0)))
    column_scales = 0.25 * spread * jnp.exp(jnp.log(3.0) * position)
    matrix = noise * column_scales[None, :]
    return jnp.clip(matrix, -2.0, 2.0).astype(jnp.bfloat16)


def set_ends(values, key, least, top_value):
    place = [jax.random.randint(jax.random.fold_in(key, axis), (), 0, length) for axis, length in enumerate(values.shape)]
    main_axis = values.shape.index(max(values.shape))
    beside = place[:main_axis] + [(place[main_axis] + 1) % values.shape[main_axis]] + place[main_axis + 1:]
    return values.at[tuple(place)].set(least).at[tuple(beside)].set(top_value)


def shard_levels(own_key, shape, shards, low, top_value):
    loudness, own = 1.0, jax.random.fold_in(own_key, 6)
    for dim, shards_of in shards:
        steps = jnp.exp(jax.random.uniform(jax.random.fold_in(own, dim), (shards_of,), jnp.float32, low / len(shards), top_value / len(shards)))
        loudness = loudness * jnp.repeat(steps, shape[dim] // shards_of).reshape([-1 if axis == dim else 1 for axis in range(len(shape))])
    return loudness


def ranked_wide(stream_key, extent, number_of, skew):
    weights = [min(1 << octave, number_of + 1 - (1 << octave)) * (1 << 20) // math.isqrt((1 << octave) ** skew) + 1 for octave in range((number_of + 1).bit_length()) if 1 << octave <= number_of]
    scale = 1 + sum(weights) // (1 << 30)
    grid = np.cumsum(np.array([max(1, weight // scale) for weight in weights]))
    ticket = jax.random.randint(jax.random.fold_in(stream_key, 1), extent, 0, int(grid[len(weights) - 1]))
    start = jnp.left_shift(1, jnp.searchsorted(jnp.asarray(grid, jnp.int32), ticket, side="right").astype(jnp.int32))
    grade = start - 1 + jax.random.randint(jax.random.fold_in(stream_key, 4), extent, 0, 1 << 30) % jnp.minimum(start, number_of + 1 - start)
    return jax.random.permutation(jax.random.fold_in(stream_key, 2), number_of)[grade].astype(jnp.int32)


def scatter_about(key, dims, width, most, kind=jnp.bfloat16):
    return jnp.clip(width * jax.random.normal(key, dims, jnp.float32), -most, most).astype(kind)


def setup_inputs(seed: int = 0) -> dict:
    streams_of = jax.random.split(jax.random.key(seed), 9)
    return {
        "hidden": draw_hidden(jax.random.fold_in(streams_of[8], 71), 0),
        "head_weight": draw_head_weight(jax.random.fold_in(streams_of[8], 71), 0),
        "targets": set_ends(ranked_wide(streams_of[2], (TOKENS,), V, 2), jax.random.fold_in(streams_of[2], 3), 0, V - 1).astype(jnp.int32),
        "segment_ids": draw_segment_ids(jax.random.fold_in(streams_of[8], 71), 0),
        "lengths": draw_lengths(jax.random.fold_in(streams_of[8], 71), 0),
        "loss_mask": set_ends((jax.random.randint(streams_of[5], (TOKENS,), 0, 4) < 3).astype(jnp.int32), jax.random.fold_in(streams_of[5], 1), 0, 1),
        "advantages": scatter_about(streams_of[6], (N_SEQ,), 1.0, 4.0, jnp.float32),
        "ref_logprobs": jnp.clip(-40.0 + 38.0 * jax.random.uniform(streams_of[7], (TOKENS,), jnp.float32) ** shard_levels(streams_of[7], (TOKENS,), ((0, 2),), -0.2, 0.2), -40.0, -2.0),
    }


kl_weight = 0.1
entropy_weight = 0.05


def combine_stats(left_stats, right_stats):
    max_one, sum_one, logit_one, target_one = left_stats
    max_two, sum_two, logit_two, target_two = right_stats
    new_max = jnp.maximum(max_one, max_two)
    scale_one = jnp.exp(max_one - new_max)
    scale_two = jnp.exp(max_two - new_max)
    return (new_max, sum_one * scale_one + sum_two * scale_two,
            logit_one * scale_one + logit_two * scale_two, target_one + target_two)


def reference(hidden, head_weight, targets, segment_ids, lengths, loss_mask, advantages, ref_logprobs):
    block_count = N_CTX * N_VOCAB
    first_columns = jnp.arange(block_count, dtype=jnp.int32) * V_DEV

    def block_logits(first_column):
        weight_block = lax.dynamic_slice_in_dim(head_weight, first_column, V_DEV, 1)
        logits = jnp.dot(hidden, weight_block, preferred_element_type=jnp.float32)
        columns = first_column + jnp.arange(V_DEV, dtype=jnp.int32)
        target_hits = targets[:, None] == columns[None, :]
        return weight_block, logits, target_hits

    def stats_step(carry, first_column):
        weight_block, logits, target_hits = block_logits(first_column)
        local_max = jnp.max(logits, axis=1)
        shifted = jnp.exp(logits - local_max[:, None])
        stats = (local_max, jnp.sum(shifted, axis=1), jnp.sum(shifted * logits, axis=1),
                 jnp.sum(jnp.where(target_hits, logits, 0.0), axis=1))
        return combine_stats(carry, stats), None

    start_stats = (jnp.full((TOKENS,), -jnp.inf, jnp.float32), jnp.zeros((TOKENS,), jnp.float32),
                   jnp.zeros((TOKENS,), jnp.float32), jnp.zeros((TOKENS,), jnp.float32))
    stats, unused = lax.scan(stats_step, start_stats, first_columns)
    row_max, exp_total, exp_logit, target_logit = stats
    log_total = row_max + jnp.log(exp_total)
    target_logp = target_logit - log_total
    mean_logit = exp_logit / exp_total

    seq_onehot = segment_ids[:, None] == jnp.arange(N_SEQ, dtype=jnp.int32)[None, :]
    token_adv = jnp.sum(jnp.where(seq_onehot, advantages[None, :], 0.0), axis=1)
    token_len = jnp.sum(jnp.where(seq_onehot, lengths[None, :].astype(jnp.float32), 0.0), axis=1)
    token_weight = LOSS_SCALE * loss_mask.astype(jnp.float32) / token_len
    logp_grad = -token_adv + kl_weight * (target_logp - ref_logprobs)
    hidden_wide = hidden.reshape(N_DP, TOK_GRP, D).astype(jnp.float32)

    def grad_step(carry, first_column):
        weight_block, logits, target_hits = block_logits(first_column)
        probs = jnp.exp(logits - log_total[:, None])
        inner = logp_grad[:, None] * (target_hits.astype(jnp.float32) - probs)
        inner = inner + entropy_weight * probs * (logits - mean_logit[:, None])
        grad_logits = (token_weight[:, None] * inner).astype(jnp.bfloat16)
        carry = carry + jnp.dot(grad_logits, weight_block.T, preferred_element_type=jnp.float32)
        halves = jnp.einsum("gtd,gtv->gdv", hidden_wide,
                            grad_logits.reshape(N_DP, TOK_GRP, V_DEV).astype(jnp.float32))
        halves = lax.optimization_barrier(halves.astype(jnp.bfloat16)).astype(jnp.float32)
        return carry, jnp.sum(halves, axis=0).astype(jnp.bfloat16)

    grad_rows, head_blocks = lax.scan(grad_step, jnp.zeros((TOKENS, D), jnp.float32), first_columns)
    grad_head = jnp.transpose(head_blocks, (1, 0, 2)).reshape(D, V)
    return grad_rows.astype(jnp.bfloat16), grad_head
```

```python
import jax
import jax.numpy as jnp
from jax import lax
from jax.sharding import Mesh, PartitionSpec as P

LOSS_SCALE = 1024
KL_WEIGHT = 0.1
ENTROPY_WEIGHT = 0.05


def combine(parts):
    top = parts[0][0]
    for part in parts[1:]:
        top = jnp.maximum(top, part[0])
    scales = [jnp.exp(part[0] - top) for part in parts]
    total = sum(part[1] * scale for part, scale in zip(parts, scales))
    logit = sum(part[2] * scale for part, scale in zip(parts, scales))
    target = sum(part[3] for part in parts)
    return jnp.stack([top, total, logit, target])


def exchange(stats, axis):
    size = lax.axis_size(axis)
    others = [
        lax.ppermute(stats, axis, [(i, (i + step) % size) for i in range(size)])
        for step in range(1, size)
    ]
    return combine([stats] + others)


def scatter_sum(parts, axis):
    got = lax.all_to_all(parts, axis, 0, 0, tiled=True)
    return jnp.sum(got.astype(jnp.float32), axis=0)


def per_device(
    hidden, head_weight, targets, segment_ids, lengths, loss_mask, advantages, ref_logprobs
):
    bf16, f32 = jnp.bfloat16, jnp.float32
    width = head_weight.shape[1]
    depth = head_weight.shape[0]
    group = targets.shape[0]
    nz, ncore = lax.axis_size("z"), lax.axis_size("core")
    nv = lax.axis_size("x") * lax.axis_size("y")
    first_column = lax.axis_index(("z", "core", "x", "y")) * width

    seq_onehot = segment_ids[:, None] == lax.iota(jnp.int32, advantages.shape[0])[None, :]
    token_adv = jnp.sum(jnp.where(seq_onehot, advantages[None, :], 0.0), axis=1)
    token_len = jnp.sum(jnp.where(seq_onehot, lengths[None, :].astype(f32), 0.0), axis=1)
    token_weight = LOSS_SCALE * loss_mask.astype(f32) / token_len
    own = jnp.stack([token_adv, token_weight, ref_logprobs, targets.astype(f32)])
    other = lax.ppermute(own, "dp", [(0, 1), (1, 0)])
    first = lax.axis_index("dp") == 0
    both = jnp.concatenate(
        [jnp.where(first, own, other), jnp.where(first, other, own)], axis=1
    )
    adv_all, weight_all, ref_all = both[0], both[1], both[2]
    targets_all = both[3].astype(jnp.int32)

    gathered = lax.all_gather(hidden, ("dp", "z", "core"), axis=0, tiled=True)
    logits = jnp.dot(gathered, head_weight, preferred_element_type=f32)
    columns = first_column + lax.iota(jnp.int32, width)
    hits = targets_all[:, None] == columns[None, :]
    local_max = jnp.max(logits, axis=1)
    shifted = jnp.exp(logits - local_max[:, None])
    stats = jnp.stack(
        [
            local_max,
            jnp.sum(shifted, axis=1),
            jnp.sum(shifted * logits, axis=1),
            jnp.sum(jnp.where(hits, logits, 0.0), axis=1),
        ]
    )
    for axis in ("core", "y", "x", "z"):
        stats = exchange(stats, axis)
    row_max, exp_total, exp_logit, target_logit = stats[0], stats[1], stats[2], stats[3]
    log_total = row_max + jnp.log(exp_total)
    target_logp = target_logit - log_total
    mean_logit = exp_logit / exp_total
    probs = jnp.exp(logits - log_total[:, None])
    logp_grad = -adv_all + KL_WEIGHT * (target_logp - ref_all)
    inner = logp_grad[:, None] * (hits.astype(f32) - probs)
    inner = inner + ENTROPY_WEIGHT * probs * (logits - mean_logit[:, None])
    grad_logits = (weight_all[:, None] * inner).astype(bf16)

    mine = lax.dynamic_slice_in_dim(grad_logits, lax.axis_index("dp") * group, group, 0)
    rows = group // (nz * ncore * nv)
    mine = mine.reshape(nz, ncore, nv, rows, width).transpose(1, 2, 0, 3, 4).reshape(group, width)
    partial = lax.dot_general(
        mine, head_weight, (((1,), (1,)), ((), ())), preferred_element_type=f32
    ).astype(bf16)
    partial = scatter_sum(partial.reshape(ncore, -1, depth), "core").astype(bf16)
    partial = scatter_sum(partial.reshape(nv, -1, depth), ("x", "y")).astype(bf16)
    grad_hidden = scatter_sum(partial.reshape(nz, rows, depth), "z").astype(bf16)

    grad_head = lax.dot_general(
        gathered, grad_logits, (((0,), (0,)), ((), ())), preferred_element_type=f32
    ).astype(bf16)
    return grad_hidden, grad_head


def solution(mesh):
    devices = mesh.devices.reshape(2, 4, 2, 4, 4)
    fine = Mesh(devices, ("dp", "z", "core", "x", "y"))
    ctx, vocab = ("z", "core"), ("x", "y")
    return jax.shard_map(
        per_device,
        mesh=fine,
        in_specs=(
            P(("dp",) + ctx, None),
            P(None, ctx + vocab),
            P("dp"),
            P("dp"),
            P(),
            P("dp"),
            P(),
            P("dp"),
        ),
        out_specs=(P(("dp",) + ctx + vocab, None), P(None, ctx + vocab)),
        check_vma=False,
    )
```

```python
import jax
import jax.numpy as jnp
from jax import lax
from jax.sharding import Mesh, PartitionSpec as P

LOSS_SCALE = 1024
KL_WEIGHT = 0.1
ENTROPY_WEIGHT = 0.05


def combine(parts):
    top = parts[0][0]
    for part in parts[1:]:
        top = jnp.maximum(top, part[0])
    scales = [jnp.exp(part[0] - top) for part in parts]
    total = sum(part[1] * scale for part, scale in zip(parts, scales))
    logit = sum(part[2] * scale for part, scale in zip(parts, scales))
    target = sum(part[3] for part in parts)
    return jnp.stack([top, total, logit, target])


def exchange(stats, axis):
    size = lax.axis_size(axis)
    others = [
        lax.ppermute(stats, axis, [(i, (i + step) % size) for i in range(size)])
        for step in range(1, size)
    ]
    return combine([stats] + others)


def scatter_sum(parts, axis):
    got = lax.all_to_all(parts, axis, 0, 0, tiled=True)
    return jnp.sum(got.astype(jnp.float32), axis=0)


def swap(value, axis):
    return lax.ppermute(value, axis, [(0, 1), (1, 0)])


def per_device(
    hidden, head_weight, targets, segment_ids, lengths, loss_mask, advantages, ref_logprobs
):
    bf16, f32 = jnp.bfloat16, jnp.float32
    depth, width = head_weight.shape
    nz, ncore = lax.axis_size("z"), lax.axis_size("core")
    nv = lax.axis_size("x") * lax.axis_size("y")
    block = hidden.shape[0]
    z, core, place = lax.axis_index("z"), lax.axis_index("core"), lax.axis_index(("x", "y"))

    weights = [head_weight, swap(head_weight, "core")]
    gathered = lax.all_gather(hidden, ("dp", "z"), axis=0, tiled=True)
    first_columns = [((z * ncore + c) * nv + place) * width for c in (core, 1 - core)]

    seq_onehot = segment_ids[:, None] == lax.iota(jnp.int32, advantages.shape[0])[None, :]
    token_adv = jnp.sum(jnp.where(seq_onehot, advantages[None, :], 0.0), axis=1)
    token_len = jnp.sum(jnp.where(seq_onehot, lengths[None, :].astype(f32), 0.0), axis=1)
    token_weight = LOSS_SCALE * loss_mask.astype(f32) / token_len
    own = jnp.stack([token_adv, token_weight, ref_logprobs, targets.astype(f32)])
    own = own.reshape(4, nz, ncore, block)
    own = jnp.where(core == 0, own[:, :, 0], own[:, :, 1]).reshape(4, nz * block)
    other = swap(own, "dp")
    first = lax.axis_index("dp") == 0
    both = jnp.concatenate(
        [jnp.where(first, own, other), jnp.where(first, other, own)], axis=1
    )
    adv_all, weight_all, ref_all = both[0], both[1], both[2]
    targets_all = both[3].astype(jnp.int32)

    logits = [jnp.dot(gathered, w, preferred_element_type=f32) for w in weights]
    hits = [
        targets_all[:, None] == (c + lax.iota(jnp.int32, width))[None, :] for c in first_columns
    ]
    local_max = jnp.maximum(*[jnp.max(part, axis=1) for part in logits])
    shifted = [jnp.exp(part - local_max[:, None]) for part in logits]
    stats = jnp.stack(
        [
            local_max,
            sum(jnp.sum(s, axis=1) for s in shifted),
            sum(jnp.sum(s * part, axis=1) for s, part in zip(shifted, logits)),
            sum(jnp.sum(jnp.where(h, part, 0.0), axis=1) for h, part in zip(hits, logits)),
        ]
    )
    for axis in ("y", "x", "z"):
        stats = exchange(stats, axis)
    row_max, exp_total, exp_logit, target_logit = stats[0], stats[1], stats[2], stats[3]
    log_total = row_max + jnp.log(exp_total)
    target_logp = target_logit - log_total
    mean_logit = exp_logit / exp_total
    logp_grad = -adv_all + KL_WEIGHT * (target_logp - ref_all)
    grads = []
    for part, hit in zip(logits, hits):
        probs = jnp.exp(part - log_total[:, None])
        inner = logp_grad[:, None] * (hit.astype(f32) - probs)
        inner = inner + ENTROPY_WEIGHT * probs * (part - mean_logit[:, None])
        grads.append((weight_all[:, None] * inner).astype(bf16))

    rows = block // nv
    partial = 0.0
    for grad, w in zip(grads, weights):
        mine = lax.dynamic_slice_in_dim(grad, lax.axis_index("dp") * nz * block, nz * block, 0)
        mine = mine.reshape(nz, nv, rows, width).transpose(1, 0, 2, 3).reshape(nz * block, width)
        partial = partial + lax.dot_general(
            mine, w, (((1,), (1,)), ((), ())), preferred_element_type=f32
        )
    partial = partial.astype(bf16)
    partial = scatter_sum(partial.reshape(nv, -1, depth), ("x", "y")).astype(bf16)
    grad_hidden = scatter_sum(partial.reshape(nz, rows, depth), "z").astype(bf16)

    other_hidden = swap(gathered, "core")
    other_grads = swap(grads[1], "core")
    grad_head = 0.0
    for h, g in ((gathered, grads[0]), (other_hidden, other_grads)):
        grad_head = grad_head + lax.dot_general(
            h, g, (((0,), (0,)), ((), ())), preferred_element_type=f32
        )
    return grad_hidden, grad_head.astype(bf16)


def solution(mesh):
    devices = mesh.devices.reshape(2, 4, 2, 4, 4)
    fine = Mesh(devices, ("dp", "z", "core", "x", "y"))
    ctx, vocab = ("z", "core"), ("x", "y")
    return jax.shard_map(
        per_device,
        mesh=fine,
        in_specs=(
            P(("dp",) + ctx, None),
            P(None, ctx + vocab),
            P("dp"),
            P("dp"),
            P(),
            P("dp"),
            P(),
            P("dp"),
        ),
        out_specs=(P(("dp",) + ctx + vocab, None), P(None, ctx + vocab)),
        check_vma=False,
    )
```

```python
import jax
import jax.numpy as jnp
from jax import lax
from jax.experimental import pallas as pl
from jax.experimental.pallas import tpu as pltpu
from jax.sharding import Mesh, PartitionSpec as P

LOSS_SCALE = 1024
KL_WEIGHT = 0.1
ENTROPY_WEIGHT = 0.05


def combine(parts):
    top = parts[0][0]
    for part in parts[1:]:
        top = jnp.maximum(top, part[0])
    scales = [jnp.exp(part[0] - top) for part in parts]
    total = sum(part[1] * scale for part, scale in zip(parts, scales))
    logit = sum(part[2] * scale for part, scale in zip(parts, scales))
    target = sum(part[3] for part in parts)
    return jnp.stack([top, total, logit, target])


def exchange(stats, axis):
    size = lax.axis_size(axis)
    others = [
        lax.ppermute(stats, axis, [(i, (i + step) % size) for i in range(size)])
        for step in range(1, size)
    ]
    return combine([stats] + others)


def scatter_sum(parts, axis):
    got = lax.all_to_all(parts, axis, 0, 0, tiled=True)
    return jnp.sum(got.astype(jnp.float32), axis=0)


def swap(value, axis):
    return lax.ppermute(value, axis, [(0, 1), (1, 0)])


def rows_kernel(order, grad0, grad1, weight0, weight1, out, held0, held1):
    @pl.when(pl.program_id(0) == 0)
    def _():
        for grad, held in ((grad0, held0), (grad1, held1)):
            held[...] = lax.dot_general(
                order[...], grad[...], (((1,), (1,)), ((), ())), preferred_element_type=jnp.float32
            ).astype(jnp.bfloat16)

    out[...] = (
        jnp.dot(held0[...], weight0[...], preferred_element_type=jnp.float32)
        + jnp.dot(held1[...], weight1[...], preferred_element_type=jnp.float32)
    ).astype(jnp.bfloat16)


def hidden_partial(order, grads, weights):
    width, depth = weights[0].shape
    rows, tokens = order.shape
    tile = 512
    whole = lambda *shape: pl.BlockSpec(shape, lambda i: (0, 0))
    return pl.pallas_call(
        rows_kernel,
        grid=(depth // tile,),
        in_specs=[whole(rows, tokens)]
        + [whole(width, tokens)] * 2
        + [pl.BlockSpec((width, tile), lambda i: (0, i))] * 2,
        out_specs=pl.BlockSpec((rows, tile), lambda i: (0, i)),
        out_shape=jax.ShapeDtypeStruct((rows, depth), jnp.bfloat16),
        scratch_shapes=[pltpu.VMEM((rows, width), jnp.bfloat16)] * 2,
        compiler_params=pltpu.CompilerParams(vmem_limit_bytes=32 * 2**20),
        name="grad_hidden_partial",
    )(order, *grads, *weights)


def head_kernel(*refs):
    out, half = refs[-1], (len(refs) - 1) // 2
    total = 0.0
    for grad, hidden in zip(refs[:half], refs[half:-1]):
        total = total + jnp.dot(grad[...], hidden[...], preferred_element_type=jnp.float32)
    out[...] = total.astype(jnp.bfloat16)


def head_gradient(grads, hiddens):
    width, tokens = grads[0].shape
    depth = hiddens[0].shape[1]
    tile, count = 512, len(grads)
    return pl.pallas_call(
        head_kernel,
        grid=(depth // tile,),
        in_specs=[pl.BlockSpec((width, tokens), lambda i: (0, 0))] * count
        + [pl.BlockSpec((tokens, tile), lambda i: (0, i))] * count,
        out_specs=pl.BlockSpec((width, tile), lambda i: (0, i)),
        out_shape=jax.ShapeDtypeStruct((width, depth), jnp.bfloat16),
        compiler_params=pltpu.CompilerParams(vmem_limit_bytes=32 * 2**20),
        cost_estimate=pl.CostEstimate(
            flops=2 * count * tokens * width * depth,
            bytes_accessed=2 * depth * (width + count * tokens),
            transcendentals=0,
        ),
        name="grad_head",
    )(*grads, *hiddens)


CHUNKS = 2


def per_device(
    hidden, head_weight, targets, segment_ids, lengths, loss_mask, advantages, ref_logprobs
):
    bf16, f32 = jnp.bfloat16, jnp.float32
    depth, width = head_weight.shape
    ndp, nz, ncore = lax.axis_size("dp"), lax.axis_size("z"), lax.axis_size("core")
    nv = lax.axis_size("x") * lax.axis_size("y")
    block = hidden.shape[0]
    rows = block // nv // CHUNKS
    dp, z, core = lax.axis_index("dp"), lax.axis_index("z"), lax.axis_index("core")
    place = lax.axis_index(("x", "y"))

    pieces = hidden.reshape(nv, CHUNKS, rows, depth)
    gathered = []
    for k in range(CHUNKS):
        piece = pieces[:, k].reshape(nv * rows, depth)
        if k:
            piece, gathered[-1] = lax.optimization_barrier((piece, gathered[-1]))
        gathered.append(lax.all_gather(piece, ("dp", "z"), axis=0, tiled=True))
    weights = [head_weight, swap(head_weight, "core")]
    first_columns = [((z * ncore + c) * nv + place) * width for c in (core, 1 - core)]

    seq_onehot = segment_ids[:, None] == lax.iota(jnp.int32, advantages.shape[0])[None, :]
    token_adv = jnp.sum(jnp.where(seq_onehot, advantages[None, :], 0.0), axis=1)
    token_len = jnp.sum(jnp.where(seq_onehot, lengths[None, :].astype(f32), 0.0), axis=1)
    token_weight = LOSS_SCALE * loss_mask.astype(f32) / token_len
    own = jnp.stack([token_adv, token_weight, ref_logprobs, targets.astype(f32)])
    own = own.reshape(4, nz, ncore, block)
    own = jnp.where(core == 0, own[:, :, 0], own[:, :, 1]).reshape(4, nz * block)
    other = swap(own, "dp")
    both = jnp.stack(
        [jnp.where(dp == 0, own, other), jnp.where(dp == 0, other, own)], axis=1
    ).reshape(4, ndp * nz * nv, CHUNKS, rows)

    tokens, mine = ndp * nz * nv * rows, nz * nv * rows
    row = lax.iota(jnp.int32, mine)
    source = ((dp * nz + row // rows % nz) * nv + row // (rows * nz)) * rows + row % rows
    order = (source[:, None] == lax.iota(jnp.int32, tokens)[None, :]).astype(bf16)

    sums, head_grads, head_hidden = [], [], []
    for k in range(CHUNKS):
        adv, weight, ref = [both[i, :, k].reshape(tokens) for i in range(3)]
        target = both[3, :, k].reshape(tokens).astype(jnp.int32)
        logits = [jnp.dot(gathered[k], w, preferred_element_type=f32) for w in weights]
        hits = [
            target[:, None] == (c + lax.iota(jnp.int32, width))[None, :] for c in first_columns
        ]
        local_max = jnp.maximum(*[jnp.max(part, axis=1) for part in logits])
        shifted = [jnp.exp(part - local_max[:, None]) for part in logits]
        stats = jnp.stack(
            [
                local_max,
                sum(jnp.sum(s, axis=1) for s in shifted),
                sum(jnp.sum(s * part, axis=1) for s, part in zip(shifted, logits)),
                sum(jnp.sum(jnp.where(h, part, 0.0), axis=1) for h, part in zip(hits, logits)),
            ]
        )
        for axis in ("z", "y", "x"):
            if k and axis == "y":
                stats, sums[-1] = lax.optimization_barrier((stats, sums[-1]))
            stats = exchange(stats, axis)
        row_max, exp_total, exp_logit, target_logit = stats[0], stats[1], stats[2], stats[3]
        log_total = row_max + jnp.log(exp_total)
        target_logp = target_logit - log_total
        mean_logit = exp_logit / exp_total
        logp_grad = -adv + KL_WEIGHT * (target_logp - ref)
        grads = []
        for part, hit in zip(logits, hits):
            probs = jnp.exp(part - log_total[:, None])
            inner = logp_grad[:, None] * (hit.astype(f32) - probs)
            inner = inner + ENTROPY_WEIGHT * probs * (part - mean_logit[:, None])
            grads.append((weight[:, None] * inner).astype(bf16).T)
        partial = hidden_partial(order, grads, [w.T for w in weights])
        partial, other_grads = lax.optimization_barrier((partial, swap(grads[1], "core")))
        head_grads += [grads[0], other_grads]
        head_hidden += [gathered[k], swap(gathered[k], "core")]
        if k + 1 < CHUNKS:
            gathered[k + 1], partial = lax.optimization_barrier((gathered[k + 1], partial))
        got = lax.all_to_all(
            partial.reshape(nv, nz * rows, depth), ("x", "y"), 0, 0, tiled=True
        )
        sums.append(got)

    grad_head = head_gradient(head_grads, head_hidden)
    sums[-1], grad_head = lax.optimization_barrier((sums[-1], grad_head))
    sums = [jnp.sum(got.astype(f32), axis=0).astype(bf16).reshape(nz, rows, depth) for got in sums]
    grad_hidden = scatter_sum(jnp.concatenate(sums, axis=1), "z").astype(bf16)
    return grad_hidden, grad_head.T


def solution(mesh):
    devices = mesh.devices.reshape(2, 4, 2, 4, 4)
    fine = Mesh(devices, ("dp", "z", "core", "x", "y"))
    ctx, vocab = ("z", "core"), ("x", "y")
    return jax.shard_map(
        per_device,
        mesh=fine,
        in_specs=(
            P(("dp",) + ctx, None),
            P(None, ctx + vocab),
            P("dp"),
            P("dp"),
            P(),
            P("dp"),
            P(),
            P("dp"),
        ),
        out_specs=(P(("dp",) + ctx + vocab, None), P(None, ctx + vocab)),
        check_vma=False,
    )
```

```python
import jax
import jax.numpy as jnp
from jax import lax
from jax.experimental import pallas as pl
from jax.experimental.pallas import tpu as pltpu
from jax.sharding import Mesh, PartitionSpec as P

LOSS_SCALE = 1024
KL_WEIGHT = 0.1
ENTROPY_WEIGHT = 0.05


def combine(parts):
    top = parts[0][0]
    for part in parts[1:]:
        top = jnp.maximum(top, part[0])
    scales = [jnp.exp(part[0] - top) for part in parts]
    total = sum(part[1] * scale for part, scale in zip(parts, scales))
    logit = sum(part[2] * scale for part, scale in zip(parts, scales))
    target = sum(part[3] for part in parts)
    return [top, total, logit, target]


def exchange(stats, axis):
    size = lax.axis_size(axis)
    others = [
        lax.ppermute(stats, axis, [(i, (i + step) % size) for i in range(size)])
        for step in range(1, size)
    ]
    return [stats] + others


def scatter_sum(parts, axis):
    got = lax.all_to_all(parts, axis, 0, 0, tiled=True)
    return jnp.sum(got.astype(jnp.float32), axis=0)


def swap(value, axis):
    return lax.ppermute(value, axis, [(0, 1), (1, 0)])


TILE = 512
PARAMS = pltpu.CompilerParams(vmem_limit_bytes=40 * 2**20)


def whole(*shape):
    return pl.BlockSpec(shape, lambda i: (0,) * len(shape))


def columns_of(step, straight, pieces, use):
    lead = pl.num_programs(0) // 2

    @pl.when(step < lead)
    def _():
        use([ref[...] for ref in straight])

    @pl.when(step >= lead)
    def _():
        use([jnp.concatenate([ref[j] for j in range(ref.shape[0])], axis=1) for ref in pieces])


def hidden_specs(tokens, depth, piece):
    lead = depth // TILE // 2
    return (
        pl.BlockSpec((tokens, TILE), lambda i: (0, jnp.minimum(i, lead - 1))),
        pl.BlockSpec((TILE // piece, tokens, piece), lambda i: (jnp.maximum(i - lead, 0), 0, 0)),
    )


def logits_kernel(first, target, straight, pieces, weight0, weight1, logits0, logits1, stats):
    step = pl.program_id(0)

    @pl.when(step == 0)
    def _():
        logits0[...] = jnp.zeros_like(logits0)
        logits1[...] = jnp.zeros_like(logits1)

    def use(tiles):
        for weight, logits in ((weight0, logits0), (weight1, logits1)):
            logits[...] += lax.dot_general(
                weight[...],
                tiles[0],
                (((1,), (1,)), ((), ())),
                preferred_element_type=jnp.float32,
            )

    columns_of(step, [straight], [pieces], use)

    @pl.when(step == pl.num_programs(0) - 1)
    def _():
        top = jnp.maximum(
            jnp.max(logits0[...], axis=0, keepdims=True),
            jnp.max(logits1[...], axis=0, keepdims=True),
        )
        stats[0:1, :] = top
        total, weighted, hit_sum = 0.0, 0.0, 0.0
        for k, logits in enumerate((logits0, logits1)):
            value = logits[...]
            shifted = jnp.exp(value - top)
            column = first[k] + lax.broadcasted_iota(jnp.int32, value.shape, 0)
            hit = jnp.where(column == target[...], value, 0.0)
            total += jnp.sum(shifted, axis=0, keepdims=True)
            weighted += jnp.sum(shifted * value, axis=0, keepdims=True)
            hit_sum += jnp.sum(hit, axis=0, keepdims=True)
        stats[1:2, :] = total
        stats[2:3, :] = weighted
        stats[3:4, :] = hit_sum


def logits_and_stats(first, target, straight, pieces, weights):
    width, depth = weights[0].shape
    tokens = straight.shape[0]
    return pl.pallas_call(
        logits_kernel,
        grid=(depth // TILE,),
        in_specs=[pl.BlockSpec(memory_space=pltpu.SMEM), whole(1, tokens)]
        + list(hidden_specs(tokens, depth, pieces.shape[2]))
        + [pl.BlockSpec((width, TILE), lambda i: (0, i))] * 2,
        out_specs=[whole(width, tokens)] * 2 + [whole(4, tokens)],
        out_shape=[jax.ShapeDtypeStruct((width, tokens), jnp.float32)] * 2
        + [jax.ShapeDtypeStruct((4, tokens), jnp.float32)],
        compiler_params=PARAMS,
        name="logits",
    )(first, target, straight, pieces, *weights)


def partial_kernel(
    first, target, order, info, part0, part1, part2, part3, logits0, logits1, weight0, weight1,
    out, grad0, grad1, held0, held1,
):
    @pl.when(pl.program_id(0) == 0)
    def _():
        parts = [[ref[i : i + 1, :] for i in range(4)] for ref in (part0, part1, part2, part3)]
        row_max, exp_total, exp_logit, target_logit = combine(parts)
        adv, weight, ref_logp = [info[i : i + 1, :] for i in range(3)]
        log_total = row_max + jnp.log(exp_total)
        target_logp = target_logit - log_total
        mean_logit = exp_logit / exp_total
        logp_grad = -adv + KL_WEIGHT * (target_logp - ref_logp)
        sets = ((logits0, grad0, held0), (logits1, grad1, held1))
        for k, (logits, grad, held) in enumerate(sets):
            value = logits[...]
            column = first[k] + lax.broadcasted_iota(jnp.int32, value.shape, 0)
            hit = jnp.where(column == target[...], 1.0, 0.0)
            probs = jnp.exp(value - log_total)
            inner = logp_grad * (hit - probs)
            inner = inner + ENTROPY_WEIGHT * probs * (value - mean_logit)
            result = (weight * inner).astype(jnp.bfloat16)
            grad[...] = result
            held[...] = lax.dot_general(
                order[...], result, (((1,), (1,)), ((), ())), preferred_element_type=jnp.float32
            ).astype(jnp.bfloat16)

    out[...] = (
        jnp.dot(held0[...], weight0[...], preferred_element_type=jnp.float32)
        + jnp.dot(held1[...], weight1[...], preferred_element_type=jnp.float32)
    ).astype(jnp.bfloat16)


def gradient_partial(first, target, order, info, parts, logits, weights):
    width, depth = weights[0].shape
    rows, tokens = order.shape
    return pl.pallas_call(
        partial_kernel,
        grid=(depth // TILE,),
        in_specs=[pl.BlockSpec(memory_space=pltpu.SMEM), whole(1, tokens), whole(rows, tokens)]
        + [whole(4, tokens)] * 5
        + [whole(width, tokens)] * 2
        + [pl.BlockSpec((width, TILE), lambda i: (0, i))] * 2,
        out_specs=[pl.BlockSpec((rows, TILE), lambda i: (0, i))] + [whole(width, tokens)] * 2,
        out_shape=[jax.ShapeDtypeStruct((rows, depth), jnp.bfloat16)]
        + [jax.ShapeDtypeStruct((width, tokens), jnp.bfloat16)] * 2,
        scratch_shapes=[pltpu.VMEM((rows, width), jnp.bfloat16)] * 2,
        compiler_params=PARAMS,
        name="grad_hidden_partial",
    )(first, target, order, info, *parts, *logits, *weights)


def head_kernel(grad0, grad1, straight0, pieces0, straight1, pieces1, out):
    def use(tiles):
        out[...] = (
            jnp.dot(grad0[...], tiles[0], preferred_element_type=jnp.float32)
            + jnp.dot(grad1[...], tiles[1], preferred_element_type=jnp.float32)
        ).astype(jnp.bfloat16)

    columns_of(pl.program_id(0), [straight0, straight1], [pieces0, pieces1], use)


def head_gradient(grads, hiddens):
    width, tokens = grads[0].shape
    depth = 2 * hiddens[0][0].shape[1]
    return pl.pallas_call(
        head_kernel,
        grid=(depth // TILE,),
        in_specs=[whole(width, tokens)] * 2
        + list(hidden_specs(tokens, depth, hiddens[0][1].shape[2])) * 2,
        out_specs=pl.BlockSpec((width, TILE), lambda i: (0, i)),
        out_shape=jax.ShapeDtypeStruct((width, depth), jnp.bfloat16),
        compiler_params=PARAMS,
        cost_estimate=pl.CostEstimate(
            flops=4 * tokens * width * depth,
            bytes_accessed=2 * depth * (width + 2 * tokens),
            transcendentals=0,
        ),
        name="grad_head",
    )(*grads, *hiddens[0], *hiddens[1])


def per_device(
    hidden, head_weight, targets, segment_ids, lengths, loss_mask, advantages, ref_logprobs
):
    bf16, f32 = jnp.bfloat16, jnp.float32
    depth, width = head_weight.shape
    ndp, nz, ncore = lax.axis_size("dp"), lax.axis_size("z"), lax.axis_size("core")
    nv = lax.axis_size("x") * lax.axis_size("y")
    block = hidden.shape[0]
    rows = block // nv
    dp, z, core = lax.axis_index("dp"), lax.axis_index("z"), lax.axis_index("core")
    place = lax.axis_index(("x", "y"))
    half, piece = depth // 2, depth // 2 // nv

    straight = lax.all_gather(hidden[:, :half], ("dp", "z"), axis=0, tiled=True)
    share = lax.dynamic_slice_in_dim(hidden, half + place * piece, piece, 1)
    share = lax.all_gather(share, ("dp", "z"), axis=0, tiled=True)
    pieces = lax.all_to_all(
        jnp.broadcast_to(share[None], (nv,) + share.shape), ("x", "y"), 0, 0, tiled=True
    )
    weights = [head_weight.T, swap(head_weight.T, "core")]
    first = jnp.stack([((z * ncore + c) * nv + place) * width for c in (core, 1 - core)])

    seq_onehot = segment_ids[:, None] == lax.iota(jnp.int32, advantages.shape[0])[None, :]
    token_adv = jnp.sum(jnp.where(seq_onehot, advantages[None, :], 0.0), axis=1)
    token_len = jnp.sum(jnp.where(seq_onehot, lengths[None, :].astype(f32), 0.0), axis=1)
    token_weight = LOSS_SCALE * loss_mask.astype(f32) / token_len
    own = jnp.stack([token_adv, token_weight, ref_logprobs, targets.astype(f32)])
    own = own.reshape(4, nz, ncore, block)
    own = jnp.where(core == 0, own[:, :, 0], own[:, :, 1]).reshape(4, nz * block)
    other = swap(own, "dp")
    info = jnp.concatenate(
        [jnp.where(dp == 0, own, other), jnp.where(dp == 0, other, own)], axis=1
    )
    target = info[3:4].astype(jnp.int32)

    tokens, mine = ndp * nz * block, nz * block
    row = lax.iota(jnp.int32, mine)
    source = ((dp * nz + row // rows % nz) * nv + row // (rows * nz)) * rows + row % rows
    order = (source[:, None] == lax.iota(jnp.int32, tokens)[None, :]).astype(bf16)

    *logits, stats = logits_and_stats(first, target, straight, pieces, weights)
    for axis in ("y", "x"):
        stats = jnp.stack(combine(exchange(stats, axis)))
    parts = exchange(stats, "z")
    partial, grad_own, grad_other = gradient_partial(
        first, target, order, info, parts, logits, weights
    )
    got = lax.all_to_all(partial.reshape(nv, nz * rows, depth), ("x", "y"), 0, 0, tiled=True)
    grad_head = head_gradient(
        (grad_own, swap(grad_other, "core")),
        ((straight, pieces), (swap(straight, "core"), swap(pieces, "core"))),
    )
    got, grad_head = lax.optimization_barrier((got, grad_head))
    got = jnp.sum(got.astype(f32), axis=0).astype(bf16)
    grad_hidden = scatter_sum(got.reshape(nz, rows, depth), "z").astype(bf16)
    return grad_hidden, grad_head.T


def solution(mesh):
    devices = mesh.devices.reshape(2, 4, 2, 4, 4)
    fine = Mesh(devices, ("dp", "z", "core", "x", "y"))
    ctx, vocab = ("z", "core"), ("x", "y")
    return jax.shard_map(
        per_device,
        mesh=fine,
        in_specs=(
            P(("dp",) + ctx, None),
            P(None, ctx + vocab),
            P("dp"),
            P("dp"),
            P(),
            P("dp"),
            P(),
            P("dp"),
        ),
        out_specs=(P(("dp",) + ctx + vocab, None), P(None, ctx + vocab)),
        check_vma=False,
    )
```

```python
import jax
import jax.numpy as jnp
from jax import lax
from jax.experimental import pallas as pl
from jax.experimental.pallas import tpu as pltpu
from jax.sharding import Mesh, PartitionSpec as P

LOSS_SCALE = 1024
KL_WEIGHT = 0.1
ENTROPY_WEIGHT = 0.05


def combine(parts):
    top = parts[0][0]
    for part in parts[1:]:
        top = jnp.maximum(top, part[0])
    scales = [jnp.exp(part[0] - top) for part in parts]
    total = sum(part[1] * scale for part, scale in zip(parts, scales))
    logit = sum(part[2] * scale for part, scale in zip(parts, scales))
    target = sum(part[3] for part in parts)
    return [top, total, logit, target]


def exchange(stats, axis):
    size = lax.axis_size(axis)
    others = [
        lax.ppermute(stats, axis, [(i, (i + step) % size) for i in range(size)])
        for step in range(1, size)
    ]
    return [stats] + others


def scatter_sum(parts, axis):
    got = lax.all_to_all(parts, axis, 0, 0, tiled=True)
    return jnp.sum(got.astype(jnp.float32), axis=0)


def spread(value, axis):
    count = lax.axis_size(axis)
    copies = jnp.broadcast_to(value[None], (count,) + value.shape)
    return lax.all_to_all(copies, axis, 0, 0, tiled=True)


def swap(value, axis):
    return lax.ppermute(value, axis, [(0, 1), (1, 0)])


TILE = 1024
PARAMS = pltpu.CompilerParams(vmem_limit_bytes=24 * 2**20)


def whole(*shape):
    return pl.BlockSpec(shape, lambda i: (0,) * len(shape))


def columns_of(step, straight, pieces, use):
    lead = pl.num_programs(0) // 2

    @pl.when(step < lead)
    def _():
        use([ref[...] for ref in straight])

    @pl.when(step >= lead)
    def _():
        use([jnp.concatenate([ref[j] for j in range(ref.shape[0])], axis=1) for ref in pieces])


def hidden_specs(tokens, depth, piece):
    lead = depth // TILE // 2
    return (
        pl.BlockSpec((tokens, TILE), lambda i: (0, jnp.minimum(i, lead - 1))),
        pl.BlockSpec((TILE // piece, tokens, piece), lambda i: (jnp.maximum(i - lead, 0), 0, 0)),
    )


def logits_kernel(first, target, straight, pieces, weight0, weight1, logits0, logits1, stats):
    step = pl.program_id(0)

    @pl.when(step == 0)
    def _():
        logits0[...] = jnp.zeros_like(logits0)
        logits1[...] = jnp.zeros_like(logits1)

    def use(tiles):
        for weight, logits in ((weight0, logits0), (weight1, logits1)):
            logits[...] += lax.dot_general(
                weight[...],
                tiles[0],
                (((1,), (1,)), ((), ())),
                preferred_element_type=jnp.float32,
            )

    columns_of(step, [straight], [pieces], use)

    @pl.when(step == pl.num_programs(0) - 1)
    def _():
        top = jnp.maximum(
            jnp.max(logits0[...], axis=0, keepdims=True),
            jnp.max(logits1[...], axis=0, keepdims=True),
        )
        stats[0:1, :] = top
        total, weighted, hit_sum = 0.0, 0.0, 0.0
        for k, logits in enumerate((logits0, logits1)):
            value = logits[...]
            shifted = jnp.exp(value - top)
            column = first[k] + lax.broadcasted_iota(jnp.int32, value.shape, 0)
            hit = jnp.where(column == target[...], value, 0.0)
            total += jnp.sum(shifted, axis=0, keepdims=True)
            weighted += jnp.sum(shifted * value, axis=0, keepdims=True)
            hit_sum += jnp.sum(hit, axis=0, keepdims=True)
        stats[1:2, :] = total
        stats[2:3, :] = weighted
        stats[3:4, :] = hit_sum


def logits_and_stats(first, target, straight, pieces, weights):
    width, depth = weights[0].shape
    tokens = straight.shape[0]
    return pl.pallas_call(
        logits_kernel,
        grid=(depth // TILE,),
        in_specs=[pl.BlockSpec(memory_space=pltpu.SMEM), whole(1, tokens)]
        + list(hidden_specs(tokens, depth, pieces.shape[2]))
        + [pl.BlockSpec((width, TILE), lambda i: (0, i))] * 2,
        out_specs=[whole(width, tokens)] * 2 + [whole(4, tokens)],
        out_shape=[jax.ShapeDtypeStruct((width, tokens), jnp.float32)] * 2
        + [jax.ShapeDtypeStruct((4, tokens), jnp.float32)],
        compiler_params=PARAMS,
        name="logits",
    )(first, target, straight, pieces, *weights)


def gradient_kernel(
    first, target, order, info, parts, logits0, logits1, weight0, weight1,
    out, grad0, grad1, held0, held1,
):
    @pl.when(pl.program_id(0) == 0)
    def _():
        count = parts.shape[0]
        row_max, exp_total, exp_logit, target_logit = combine(
            [[parts[j, i : i + 1, :] for i in range(4)] for j in range(count)]
        )
        adv, weight, ref_logp = [info[i : i + 1, :] for i in range(3)]
        log_total = row_max + jnp.log(exp_total)
        target_logp = target_logit - log_total
        mean_logit = exp_logit / exp_total
        logp_grad = -adv + KL_WEIGHT * (target_logp - ref_logp)
        sets = ((logits0, grad0, held0), (logits1, grad1, held1))
        for k, (logits, grad, held) in enumerate(sets):
            value = logits[...]
            column = first[k] + lax.broadcasted_iota(jnp.int32, value.shape, 0)
            hit = jnp.where(column == target[...], 1.0, 0.0)
            probs = jnp.exp(value - log_total)
            inner = logp_grad * (hit - probs)
            inner = inner + ENTROPY_WEIGHT * probs * (value - mean_logit)
            result = (weight * inner).astype(jnp.bfloat16)
            grad[...] = result
            held[...] = lax.dot_general(
                order[...], result, (((1,), (1,)), ((), ())), preferred_element_type=jnp.float32
            ).astype(jnp.bfloat16)

    out[...] = (
        jnp.dot(held0[...], weight0[...], preferred_element_type=jnp.float32)
        + jnp.dot(held1[...], weight1[...], preferred_element_type=jnp.float32)
    ).astype(jnp.bfloat16)


def gradient_partial(first, target, order, info, parts, logits, weights):
    width, depth = weights[0].shape
    rows, tokens = order.shape
    return pl.pallas_call(
        gradient_kernel,
        grid=(depth // TILE,),
        in_specs=[pl.BlockSpec(memory_space=pltpu.SMEM), whole(1, tokens), whole(rows, tokens)]
        + [whole(4, tokens), whole(*parts.shape)]
        + [whole(width, tokens)] * 2
        + [pl.BlockSpec((width, TILE), lambda i: (0, i))] * 2,
        out_specs=[pl.BlockSpec((rows, TILE), lambda i: (0, i))] + [whole(width, tokens)] * 2,
        out_shape=[pltpu.HBM((rows, depth), jnp.bfloat16)]
        + [pltpu.HBM((width, tokens), jnp.bfloat16)] * 2,
        scratch_shapes=[pltpu.VMEM((rows, width), jnp.bfloat16)] * 2,
        compiler_params=PARAMS,
        name="grad_hidden_partial",
    )(first, target, order, info, parts, *logits, *weights)


def head_kernel(grad0, grad1, straight0, pieces0, straight1, pieces1, out):
    def use(tiles):
        out[...] = (
            jnp.dot(grad0[...], tiles[0], preferred_element_type=jnp.float32)
            + jnp.dot(grad1[...], tiles[1], preferred_element_type=jnp.float32)
        ).astype(jnp.bfloat16)

    columns_of(pl.program_id(0), [straight0, straight1], [pieces0, pieces1], use)


def head_gradient(grads, hiddens):
    width, tokens = grads[0].shape
    depth = 2 * hiddens[0][0].shape[1]
    return pl.pallas_call(
        head_kernel,
        grid=(depth // TILE,),
        in_specs=[whole(width, tokens)] * 2
        + list(hidden_specs(tokens, depth, hiddens[0][1].shape[2])) * 2,
        out_specs=pl.BlockSpec((width, TILE), lambda i: (0, i)),
        out_shape=jax.ShapeDtypeStruct((width, depth), jnp.bfloat16),
        compiler_params=PARAMS,
        cost_estimate=pl.CostEstimate(
            flops=4 * tokens * width * depth,
            bytes_accessed=2 * depth * (width + 2 * tokens),
            transcendentals=0,
        ),
        name="grad_head",
    )(*grads, *hiddens[0], *hiddens[1])


def per_device(
    hidden, head_weight, targets, segment_ids, lengths, loss_mask, advantages, ref_logprobs
):
    bf16, f32 = jnp.bfloat16, jnp.float32
    depth, width = head_weight.shape
    ndp, nz, ncore = lax.axis_size("dp"), lax.axis_size("z"), lax.axis_size("core")
    nv = lax.axis_size("x") * lax.axis_size("y")
    block = hidden.shape[0]
    rows = block // nv
    dp, z, core = lax.axis_index("dp"), lax.axis_index("z"), lax.axis_index("core")
    place = lax.axis_index(("x", "y"))
    half, piece = depth // 2, depth // 2 // nv

    straight = lax.all_gather(hidden[:, :half], ("dp", "z"), axis=0, tiled=True)
    share = lax.dynamic_slice_in_dim(hidden, half + place * piece, piece, 1)
    share = spread(share, ("dp", "z")).reshape(ndp * nz * block, piece)
    pieces = spread(share, ("x", "y"))
    weights = [
        pltpu.with_memory_space_constraint(w, pltpu.HBM)
        for w in (head_weight.T, swap(head_weight.T, "core"))
    ]
    first = jnp.stack([((z * ncore + c) * nv + place) * width for c in (core, 1 - core)])

    seq_onehot = segment_ids[:, None] == lax.iota(jnp.int32, advantages.shape[0])[None, :]
    token_adv = jnp.sum(jnp.where(seq_onehot, advantages[None, :], 0.0), axis=1)
    token_len = jnp.sum(jnp.where(seq_onehot, lengths[None, :].astype(f32), 0.0), axis=1)
    token_weight = LOSS_SCALE * loss_mask.astype(f32) / token_len
    own = jnp.stack([token_adv, token_weight, ref_logprobs, targets.astype(f32)])
    own = own.reshape(4, nz, ncore, block)
    own = jnp.where(core == 0, own[:, :, 0], own[:, :, 1]).reshape(4, nz * block)
    other = swap(own, "dp")
    info = jnp.concatenate(
        [jnp.where(dp == 0, own, other), jnp.where(dp == 0, other, own)], axis=1
    )
    target = info[3:4].astype(jnp.int32)

    tokens, mine = ndp * nz * block, nz * block
    row = lax.iota(jnp.int32, mine)
    source = ((dp * nz + row // rows % nz) * nv + row // (rows * nz)) * rows + row % rows
    order = (source[:, None] == lax.iota(jnp.int32, tokens)[None, :]).astype(bf16)

    *logits, stats = logits_and_stats(first, target, straight, pieces, weights)
    stats = jnp.stack(combine(exchange(stats, "z")))
    parts = spread(stats, ("x", "y"))
    partial, grad_own, grad_other = gradient_partial(
        first, target, order, info, parts, logits, weights
    )
    got = lax.all_to_all(partial.reshape(nv, nz * rows, depth), ("x", "y"), 0, 0, tiled=True)
    grad_head = head_gradient(
        (grad_own, swap(grad_other, "core")),
        ((straight, pieces), (swap(straight, "core"), swap(pieces, "core"))),
    )
    got, grad_head = lax.optimization_barrier((got, grad_head))
    got = jnp.sum(got.astype(f32), axis=0).astype(bf16)
    grad_hidden = scatter_sum(got.reshape(nz, rows, depth), "z").astype(bf16)
    return grad_hidden, grad_head.T


def solution(mesh):
    devices = mesh.devices.reshape(2, 4, 2, 4, 4)
    fine = Mesh(devices, ("dp", "z", "core", "x", "y"))
    ctx, vocab = ("z", "core"), ("x", "y")
    return jax.shard_map(
        per_device,
        mesh=fine,
        in_specs=(
            P(("dp",) + ctx, None),
            P(None, ctx + vocab),
            P("dp"),
            P("dp"),
            P(),
            P("dp"),
            P(),
            P("dp"),
        ),
        out_specs=(P(("dp",) + ctx + vocab, None), P(None, ctx + vocab)),
        check_vma=False,
    )
```

```python
import functools

import jax
import jax.numpy as jnp
from jax import lax
from jax.experimental import pallas as pl
from jax.experimental.pallas import tpu as pltpu
from jax.sharding import Mesh, PartitionSpec as P

LOSS_SCALE = 1024
KL_WEIGHT = 0.1
ENTROPY_WEIGHT = 0.05


def combine(parts):
    top = parts[0][0]
    for part in parts[1:]:
        top = jnp.maximum(top, part[0])
    scales = [jnp.exp(part[0] - top) for part in parts]
    total = sum(part[1] * scale for part, scale in zip(parts, scales))
    logit = sum(part[2] * scale for part, scale in zip(parts, scales))
    target = sum(part[3] for part in parts)
    return [top, total, logit, target]


def exchange(stats, axis):
    size = lax.axis_size(axis)
    others = [
        lax.ppermute(stats, axis, [(i, (i + step) % size) for i in range(size)])
        for step in range(1, size)
    ]
    return [stats] + others


def scatter_sum(parts, axis):
    got = lax.all_to_all(parts, axis, 0, 0, tiled=True)
    return jnp.sum(got.astype(jnp.float32), axis=0)


def spread(value, axis):
    count = lax.axis_size(axis)
    copies = jnp.broadcast_to(value[None], (count,) + value.shape)
    return lax.all_to_all(copies, axis, 0, 0, tiled=True)


def swap(value, axis):
    return lax.ppermute(value, axis, [(0, 1), (1, 0)])


TILE = 1024
PARAMS = pltpu.CompilerParams(vmem_limit_bytes=24 * 2**20)


def whole(*shape):
    return pl.BlockSpec(shape, lambda i, s: (0,) * len(shape))


def tiles(rows):
    return pl.BlockSpec((rows, TILE), lambda i, s: (0, i))


def hidden_specs(tokens, depth, group):
    lead = depth // TILE // 2
    return [
        pl.BlockSpec((tokens, TILE), lambda i, s: (s[group], jnp.minimum(i, lead - 1))),
        pl.BlockSpec((tokens, TILE), lambda i, s: (s[group], jnp.maximum(i - lead, 0))),
    ]


def call(kernel, name, depth, in_specs, out_specs, out_shape, scratch=(), flops=0):
    return pl.pallas_call(
        kernel,
        grid_spec=pltpu.PrefetchScalarGridSpec(
            num_scalar_prefetch=1,
            grid=(depth // TILE,),
            in_specs=in_specs,
            out_specs=out_specs,
            scratch_shapes=list(scratch),
        ),
        out_shape=out_shape,
        compiler_params=PARAMS,
        cost_estimate=pl.CostEstimate(flops=flops, bytes_accessed=flops // 500, transcendentals=0),
        name=name,
    )


def halves(use_first, use_second):
    step, lead = pl.program_id(0), pl.num_programs(0) // 2
    pl.when(step < lead)(use_first)
    pl.when(step >= lead)(use_second)


def add_logits(tile, weights, logits):
    for weight, out in zip(weights, logits):
        out[...] += lax.dot_general(
            weight[...], tile, (((1,), (1,)), ((), ())), preferred_element_type=jnp.float32
        )


def hits(value, first, target):
    return first + lax.broadcasted_iota(jnp.int32, value.shape, 0) == target[...]


def logits_kernel(s, target, straight, pieces, weight0, weight1, logits0, logits1, stats):
    step = pl.program_id(0)

    @pl.when(step == 0)
    def _():
        logits0[...] = jnp.zeros_like(logits0)
        logits1[...] = jnp.zeros_like(logits1)

    def use_second():
        tile = jnp.concatenate([pieces[j] for j in range(pieces.shape[0])], axis=1)
        add_logits(tile, (weight0, weight1), (logits0, logits1))

    halves(
        lambda: add_logits(straight[...], (weight0, weight1), (logits0, logits1)), use_second
    )

    @pl.when(step == pl.num_programs(0) - 1)
    def _():
        top = jnp.maximum(
            jnp.max(logits0[...], axis=0, keepdims=True),
            jnp.max(logits1[...], axis=0, keepdims=True),
        )
        stats[0:1, :] = top
        total, weighted, hit_sum = 0.0, 0.0, 0.0
        for k, logits in enumerate((logits0, logits1)):
            value = logits[...]
            shifted = jnp.exp(value - top)
            hit = jnp.where(hits(value, s[2 + k], target), value, 0.0)
            total += jnp.sum(shifted, axis=0, keepdims=True)
            weighted += jnp.sum(shifted * value, axis=0, keepdims=True)
            hit_sum += jnp.sum(hit, axis=0, keepdims=True)
        stats[1:2, :] = total
        stats[2:3, :] = weighted
        stats[3:4, :] = hit_sum


def logits_and_stats(scalars, target, straight, pieces, weights):
    width, depth = weights[0].shape
    tokens, piece = pieces.shape[1:]
    lead = depth // TILE // 2
    return call(
        logits_kernel,
        "logits",
        depth,
        [
            whole(1, tokens),
            hidden_specs(tokens, depth, 0)[0],
            pl.BlockSpec(
                (TILE // piece, tokens, piece), lambda i, s: (jnp.maximum(i - lead, 0), 0, 0)
            ),
            tiles(width),
            tiles(width),
        ],
        [whole(width, tokens)] * 2 + [whole(4, tokens)],
        [pltpu.HBM((width, tokens), jnp.float32)] * 2
        + [jax.ShapeDtypeStruct((4, tokens), jnp.float32)],
        flops=4 * tokens * width * depth,
    )(scalars, target, straight, pieces, *weights)


def logit_gradient(value, first, target, info, final):
    adv, weight, ref_logp = [info[i : i + 1, :] for i in range(3)]
    log_total, target_logp, mean_logit = final
    logp_grad = -adv + KL_WEIGHT * (target_logp - ref_logp)
    hit = jnp.where(hits(value, first, target), 1.0, 0.0)
    probs = jnp.exp(value - log_total)
    inner = logp_grad * (hit - probs)
    inner = inner + ENTROPY_WEIGHT * probs * (value - mean_logit)
    return (weight * inner).astype(jnp.bfloat16)


def gradient_kernel(
    s, target, info, parts, logits0, logits1, weight0, weight1,
    out, grad0, grad1, final, held0, held1, *, nz, nv,
):
    @pl.when(pl.program_id(0) == 0)
    def _():
        count, tokens = parts.shape[0], parts.shape[2]
        row_max, exp_total, exp_logit, target_logit = combine(
            [[parts[j, i : i + 1, :] for i in range(4)] for j in range(count)]
        )
        log_total = row_max + jnp.log(exp_total)
        ends = (log_total, target_logit - log_total, exp_logit / exp_total)
        for i, end in enumerate(ends):
            final[i : i + 1, :] = end
        rows = tokens // (nz * nv)
        row = lax.broadcasted_iota(jnp.int32, (tokens, tokens), 0)
        token = lax.broadcasted_iota(jnp.int32, (tokens, tokens), 1)
        source = (row // rows % nz * nv + row // (rows * nz)) * rows + row % rows
        order = jnp.where(token == source, 1.0, 0.0).astype(jnp.bfloat16)
        sets = ((logits0, grad0, held0), (logits1, grad1, held1))
        for k, (logits, grad, held) in enumerate(sets):
            result = logit_gradient(logits[...], s[2 + k], target, info, ends)
            grad[...] = result
            held[...] = lax.dot_general(
                order, result, (((1,), (1,)), ((), ())), preferred_element_type=jnp.float32
            ).astype(jnp.bfloat16)

    out[...] = (
        jnp.dot(held0[...], weight0[...], preferred_element_type=jnp.float32)
        + jnp.dot(held1[...], weight1[...], preferred_element_type=jnp.float32)
    ).astype(jnp.bfloat16)


def gradient_partial(scalars, target, info, parts, logits, weights, nz, nv):
    width, depth = weights[0].shape
    tokens = info.shape[1]
    return call(
        functools.partial(gradient_kernel, nz=nz, nv=nv),
        "grad_hidden_partial",
        depth,
        [whole(1, tokens), whole(4, tokens), whole(*parts.shape)]
        + [whole(width, tokens)] * 2
        + [tiles(width)] * 2,
        [tiles(tokens)] + [whole(width, tokens)] * 2 + [whole(3, tokens)],
        [pltpu.HBM((tokens, depth), jnp.bfloat16)]
        + [pltpu.HBM((width, tokens), jnp.bfloat16)] * 2
        + [jax.ShapeDtypeStruct((3, tokens), jnp.float32)],
        [pltpu.VMEM((tokens, width), jnp.bfloat16)] * 2,
        flops=4 * tokens * width * depth,
    )(scalars, target, info, parts, *logits, *weights)


def other_kernel(
    s, target, info, final, straight, straight2, weight0, weight1, grad0, grad1, logits0, logits1
):
    step = pl.program_id(0)

    @pl.when(step == 0)
    def _():
        logits0[...] = jnp.zeros_like(logits0)
        logits1[...] = jnp.zeros_like(logits1)

    halves(
        lambda: add_logits(straight[...], (weight0, weight1), (logits0, logits1)),
        lambda: add_logits(straight2[...], (weight0, weight1), (logits0, logits1)),
    )

    @pl.when(step == pl.num_programs(0) - 1)
    def _():
        ends = [final[i : i + 1, :] for i in range(3)]
        for k, (logits, grad) in enumerate(((logits0, grad0), (logits1, grad1))):
            grad[...] = logit_gradient(logits[...], s[2 + k], target, info, ends)


def other_gradient(scalars, target, info, final, straights, weights):
    width, depth = weights[0].shape
    tokens = info.shape[1]
    return call(
        other_kernel,
        "other_group_grad_logits",
        depth,
        [whole(1, tokens), whole(4, tokens), whole(3, tokens)]
        + hidden_specs(tokens, depth, 1)
        + [tiles(width)] * 2,
        [whole(width, tokens)] * 2,
        [pltpu.HBM((width, tokens), jnp.bfloat16)] * 2,
        [pltpu.VMEM((width, tokens), jnp.float32)] * 2,
        flops=4 * tokens * width * depth,
    )(scalars, target, info, final, *straights, *weights)


def head_kernel(s, *refs):
    out, count = refs[-1], (len(refs) - 1) // 3
    grads, firsts, seconds = refs[:count], refs[count:-1:2], refs[count + 1 : -1 : 2]

    def use(hiddens):
        total = 0.0
        for grad, hidden in zip(grads, hiddens):
            total = total + jnp.dot(grad[...], hidden[...], preferred_element_type=jnp.float32)
        out[...] = total.astype(jnp.bfloat16)

    halves(lambda: use(firsts), lambda: use(seconds))


def head_gradient(scalars, grads, hiddens):
    width, tokens = grads[0].shape
    depth = 2 * hiddens[0][0].shape[1]
    return call(
        head_kernel,
        "grad_head",
        depth,
        [whole(width, tokens)] * 4
        + (hidden_specs(tokens, depth, 0) + hidden_specs(tokens, depth, 1)) * 2,
        tiles(width),
        jax.ShapeDtypeStruct((width, depth), jnp.bfloat16),
        flops=8 * tokens * width * depth,
    )(scalars, *grads, *[h for pair in hiddens for h in (*pair, *pair)])


def in_hbm(value):
    return pltpu.with_memory_space_constraint(value, pltpu.HBM)


def per_device(
    hidden, head_weight, targets, segment_ids, lengths, loss_mask, advantages, ref_logprobs
):
    bf16, f32 = jnp.bfloat16, jnp.float32
    depth, width = head_weight.shape
    nz, ncore = lax.axis_size("z"), lax.axis_size("core")
    nv = lax.axis_size("x") * lax.axis_size("y")
    block = hidden.shape[0]
    rows = block // nv
    dp, z, core = lax.axis_index("dp"), lax.axis_index("z"), lax.axis_index("core")
    place = lax.axis_index(("x", "y"))
    half, piece = depth // 2, depth // 2 // nv

    straight = lax.all_gather(hidden[:, :half], ("dp", "z"), axis=0, tiled=True)
    share = lax.dynamic_slice_in_dim(hidden, half + place * piece, piece, 1)
    share = spread(share, "z").reshape(nz * block, piece)
    pieces = spread(share, ("x", "y"))
    weights = [in_hbm(w) for w in (head_weight.T, swap(head_weight.T, "core"))]
    scalars = jnp.stack(
        [dp, 1 - dp] + [((z * ncore + c) * nv + place) * width for c in (core, 1 - core)]
    )

    seq_onehot = segment_ids[:, None] == lax.iota(jnp.int32, advantages.shape[0])[None, :]
    token_adv = jnp.sum(jnp.where(seq_onehot, advantages[None, :], 0.0), axis=1)
    token_len = jnp.sum(jnp.where(seq_onehot, lengths[None, :].astype(f32), 0.0), axis=1)
    token_weight = LOSS_SCALE * loss_mask.astype(f32) / token_len
    own = jnp.stack([token_adv, token_weight, ref_logprobs, targets.astype(f32)])
    own = own.reshape(4, nz, ncore, block)
    own = jnp.where(core == 0, own[:, :, 0], own[:, :, 1]).reshape(4, nz * block)
    other = swap(own, "dp")
    later, straight, pieces, other = lax.optimization_barrier(
        (hidden[:, half:], straight, pieces, other)
    )
    straight2 = lax.all_gather(later, ("dp", "z"), axis=0, tiled=True)
    own_target, other_target = own[3:4].astype(jnp.int32), other[3:4].astype(jnp.int32)

    *logits, stats = logits_and_stats(
        scalars, own_target, in_hbm(straight), pieces, weights
    )
    stats = jnp.stack(combine(exchange(stats, "z")))
    parts = spread(stats, ("x", "y"))
    logits = [in_hbm(value) for value in logits]
    partial, own0, own1, final = gradient_partial(
        scalars, own_target, own, parts, logits, weights, nz, nv
    )
    got = lax.all_to_all(partial.reshape(nv, nz * rows, depth), ("x", "y"), 0, 0, tiled=True)
    straight, straight2, final = lax.optimization_barrier(
        (straight, straight2, swap(final, "dp"))
    )
    gathered = (in_hbm(straight), in_hbm(straight2))
    other0, other1 = other_gradient(
        scalars, other_target, other, final, gathered, weights
    )
    grad_head = head_gradient(
        scalars,
        (own0, other0, swap(own1, "core"), swap(other1, "core")),
        (gathered, (in_hbm(swap(straight, "core")), in_hbm(swap(straight2, "core")))),
    )
    got, grad_head = lax.optimization_barrier((got, grad_head))
    got = jnp.sum(got.astype(f32), axis=0).astype(bf16)
    grad_hidden = scatter_sum(got.reshape(nz, rows, depth), "z").astype(bf16)
    return grad_hidden, grad_head.T


def solution(mesh):
    devices = mesh.devices.reshape(2, 4, 2, 4, 4)
    fine = Mesh(devices, ("dp", "z", "core", "x", "y"))
    ctx, vocab = ("z", "core"), ("x", "y")
    return jax.shard_map(
        per_device,
        mesh=fine,
        in_specs=(
            P(("dp",) + ctx, None),
            P(None, ctx + vocab),
            P("dp"),
            P("dp"),
            P(),
            P("dp"),
            P(),
            P("dp"),
        ),
        out_specs=(P(("dp",) + ctx + vocab, None), P(None, ctx + vocab)),
        check_vma=False,
    )
```

```python
import functools

import jax
import jax.numpy as jnp
from jax import lax
from jax.experimental import pallas as pl
from jax.experimental.pallas import tpu as pltpu
from jax.sharding import Mesh, PartitionSpec as P

LOSS_SCALE = 1024
KL_WEIGHT = 0.1
ENTROPY_WEIGHT = 0.05


def combine(parts):
    top = parts[0][0]
    for part in parts[1:]:
        top = jnp.maximum(top, part[0])
    scales = [jnp.exp(part[0] - top) for part in parts]
    total = sum(part[1] * scale for part, scale in zip(parts, scales))
    logit = sum(part[2] * scale for part, scale in zip(parts, scales))
    target = sum(part[3] for part in parts)
    return [top, total, logit, target]


def exchange(stats, axis):
    size = lax.axis_size(axis)
    others = [
        lax.ppermute(stats, axis, [(i, (i + step) % size) for i in range(size)])
        for step in range(1, size)
    ]
    return [stats] + others


def scatter_sum(parts, axis):
    got = lax.all_to_all(parts, axis, 0, 0, tiled=True)
    return jnp.sum(got.astype(jnp.float32), axis=0)


def spread(value, axis):
    count = lax.axis_size(axis)
    copies = jnp.broadcast_to(value[None], (count,) + value.shape)
    return lax.all_to_all(copies, axis, 0, 0, tiled=True)


def swap(value, axis):
    return lax.ppermute(value, axis, [(0, 1), (1, 0)])


TILE = 1024
PARAMS = pltpu.CompilerParams(vmem_limit_bytes=24 * 2**20)


def whole(*shape):
    return pl.BlockSpec(shape, lambda i, s: (0,) * len(shape))


def tiles(rows):
    return pl.BlockSpec((rows, TILE), lambda i, s: (0, i))


def hidden_specs(tokens, depth, group):
    lead = depth // TILE // 2
    return [
        pl.BlockSpec((tokens, TILE), lambda i, s: (s[group], jnp.minimum(i, lead - 1))),
        pl.BlockSpec((tokens, TILE), lambda i, s: (s[group], jnp.maximum(i - lead, 0))),
    ]


def call(kernel, name, depth, in_specs, out_specs, out_shape, scratch=(), flops=0):
    return pl.pallas_call(
        kernel,
        grid_spec=pltpu.PrefetchScalarGridSpec(
            num_scalar_prefetch=1,
            grid=(depth // TILE,),
            in_specs=in_specs,
            out_specs=out_specs,
            scratch_shapes=list(scratch),
        ),
        out_shape=out_shape,
        compiler_params=PARAMS,
        cost_estimate=pl.CostEstimate(flops=flops, bytes_accessed=flops // 500, transcendentals=0),
        name=name,
    )


def halves(use_first, use_second):
    step, lead = pl.program_id(0), pl.num_programs(0) // 2
    pl.when(step < lead)(use_first)
    pl.when(step >= lead)(use_second)


def add_logits(tile, weights, logits):
    for weight, out in zip(weights, logits):
        out[...] += lax.dot_general(
            weight[...], tile, (((1,), (1,)), ((), ())), preferred_element_type=jnp.float32
        )


def hits(value, first, target):
    return first + lax.broadcasted_iota(jnp.int32, value.shape, 0) == target[...]


def logits_kernel(s, target, straight, pieces, weight0, weight1, logits0, logits1, stats):
    step = pl.program_id(0)

    @pl.when(step == 0)
    def _():
        logits0[...] = jnp.zeros_like(logits0)
        logits1[...] = jnp.zeros_like(logits1)

    def use_second():
        tile = jnp.concatenate([pieces[j] for j in range(pieces.shape[0])], axis=1)
        add_logits(tile, (weight0, weight1), (logits0, logits1))

    halves(
        lambda: add_logits(straight[...], (weight0, weight1), (logits0, logits1)), use_second
    )

    @pl.when(step == pl.num_programs(0) - 1)
    def _():
        top = jnp.maximum(
            jnp.max(logits0[...], axis=0, keepdims=True),
            jnp.max(logits1[...], axis=0, keepdims=True),
        )
        stats[0:1, :] = top
        total, weighted, hit_sum = 0.0, 0.0, 0.0
        for k, logits in enumerate((logits0, logits1)):
            value = logits[...]
            shifted = jnp.exp(value - top)
            hit = jnp.where(hits(value, s[2 + k], target), value, 0.0)
            total += jnp.sum(shifted, axis=0, keepdims=True)
            weighted += jnp.sum(shifted * value, axis=0, keepdims=True)
            hit_sum += jnp.sum(hit, axis=0, keepdims=True)
        stats[1:2, :] = total
        stats[2:3, :] = weighted
        stats[3:4, :] = hit_sum


def logits_and_stats(scalars, target, straight, pieces, weights):
    width, depth = weights[0].shape
    tokens, piece = pieces.shape[1:]
    lead = depth // TILE // 2
    return call(
        logits_kernel,
        "logits",
        depth,
        [
            whole(1, tokens),
            hidden_specs(tokens, depth, 0)[0],
            pl.BlockSpec(
                (TILE // piece, tokens, piece), lambda i, s: (jnp.maximum(i - lead, 0), 0, 0)
            ),
            tiles(width),
            tiles(width),
        ],
        [whole(width, tokens)] * 2 + [whole(4, tokens)],
        [pltpu.HBM((width, tokens), jnp.float32)] * 2
        + [jax.ShapeDtypeStruct((4, tokens), jnp.float32)],
        flops=4 * tokens * width * depth,
    )(scalars, target, straight, pieces, *weights)


def logit_gradient(value, first, target, info, final):
    adv, weight, ref_logp = [info[i : i + 1, :] for i in range(3)]
    log_total, target_logp, mean_logit = final
    logp_grad = -adv + KL_WEIGHT * (target_logp - ref_logp)
    hit = jnp.where(hits(value, first, target), 1.0, 0.0)
    probs = jnp.exp(value - log_total)
    inner = logp_grad * (hit - probs)
    inner = inner + ENTROPY_WEIGHT * probs * (value - mean_logit)
    return (weight * inner).astype(jnp.bfloat16)


def gradient_kernel(
    s, target, info, parts, logits0, logits1, weight0, weight1,
    out, grad0, grad1, final, held0, held1, *, nz, nv,
):
    @pl.when(pl.program_id(0) == 0)
    def _():
        count, tokens = parts.shape[0], parts.shape[2]
        row_max, exp_total, exp_logit, target_logit = combine(
            [[parts[j, i : i + 1, :] for i in range(4)] for j in range(count)]
        )
        log_total = row_max + jnp.log(exp_total)
        ends = (log_total, target_logit - log_total, exp_logit / exp_total)
        for i, end in enumerate(ends):
            final[i : i + 1, :] = end
        rows = tokens // (nz * nv)
        row = lax.broadcasted_iota(jnp.int32, (tokens, tokens), 0)
        token = lax.broadcasted_iota(jnp.int32, (tokens, tokens), 1)
        source = (row // rows % nz * nv + row // (rows * nz)) * rows + row % rows
        order = jnp.where(token == source, 1.0, 0.0).astype(jnp.bfloat16)
        sets = ((logits0, grad0, held0), (logits1, grad1, held1))
        for k, (logits, grad, held) in enumerate(sets):
            result = logit_gradient(logits[...], s[2 + k], target, info, ends)
            grad[...] = result
            held[...] = lax.dot_general(
                order, result, (((1,), (1,)), ((), ())), preferred_element_type=jnp.float32
            ).astype(jnp.bfloat16)

    out[...] = (
        jnp.dot(held0[...], weight0[...], preferred_element_type=jnp.float32)
        + jnp.dot(held1[...], weight1[...], preferred_element_type=jnp.float32)
    ).astype(jnp.bfloat16)


def gradient_partial(scalars, target, info, parts, logits, weights, nz, nv):
    width, depth = weights[0].shape
    tokens = info.shape[1]
    return call(
        functools.partial(gradient_kernel, nz=nz, nv=nv),
        "grad_hidden_partial",
        depth,
        [whole(1, tokens), whole(4, tokens), whole(*parts.shape)]
        + [whole(width, tokens)] * 2
        + [tiles(width)] * 2,
        [tiles(tokens)] + [whole(width, tokens)] * 2 + [whole(3, tokens)],
        [pltpu.HBM((tokens, depth), jnp.bfloat16)]
        + [pltpu.HBM((width, tokens), jnp.bfloat16)] * 2
        + [jax.ShapeDtypeStruct((3, tokens), jnp.float32)],
        [pltpu.VMEM((tokens, width), jnp.bfloat16)] * 2,
        flops=4 * tokens * width * depth,
    )(scalars, target, info, parts, *logits, *weights)


def other_kernel(
    s, target, info, final, straight, straight2, weight0, weight1, grad0, grad1, logits0, logits1
):
    step = pl.program_id(0)

    @pl.when(step == 0)
    def _():
        logits0[...] = jnp.zeros_like(logits0)
        logits1[...] = jnp.zeros_like(logits1)

    halves(
        lambda: add_logits(straight[...], (weight0, weight1), (logits0, logits1)),
        lambda: add_logits(straight2[...], (weight0, weight1), (logits0, logits1)),
    )

    @pl.when(step == pl.num_programs(0) - 1)
    def _():
        ends = [final[i : i + 1, :] for i in range(3)]
        for k, (logits, grad) in enumerate(((logits0, grad0), (logits1, grad1))):
            grad[...] = logit_gradient(logits[...], s[2 + k], target, info, ends)


def other_gradient(scalars, target, info, final, straights, weights):
    width, depth = weights[0].shape
    tokens = info.shape[1]
    return call(
        other_kernel,
        "other_group_grad_logits",
        depth,
        [whole(1, tokens), whole(4, tokens), whole(3, tokens)]
        + hidden_specs(tokens, depth, 1)
        + [tiles(width)] * 2,
        [whole(width, tokens)] * 2,
        [pltpu.HBM((width, tokens), jnp.bfloat16)] * 2,
        [pltpu.VMEM((width, tokens), jnp.float32)] * 2,
        flops=4 * tokens * width * depth,
    )(scalars, target, info, final, *straights, *weights)


def head_kernel(s, *refs, count):
    out, total = refs[-1], 0.0
    for grad, hidden in zip(refs[:count], refs[count : 2 * count]):
        total = total + jnp.dot(grad[...], hidden[...], preferred_element_type=jnp.float32)
    out[...] = total.astype(jnp.bfloat16)


def head_half(scalars, grads, hiddens, before=None):
    width, tokens = grads[0].shape
    half = hiddens[0].shape[1]
    steps = half // TILE
    skip = 0 if before is None else steps
    extra = [] if before is None else [before]
    rows = [pl.BlockSpec((tokens, TILE), lambda i, s, g=g: (s[g], i)) for g in (0, 1)]
    return pl.pallas_call(
        functools.partial(head_kernel, count=4),
        grid_spec=pltpu.PrefetchScalarGridSpec(
            num_scalar_prefetch=1,
            grid=(steps,),
            in_specs=[whole(width, tokens)] * 4
            + rows * 2
            + [pl.BlockSpec(memory_space=pl.ANY)] * len(extra),
            out_specs=pl.BlockSpec((width, TILE), lambda i, s: (0, i + skip)),
        ),
        out_shape=pltpu.HBM((width, 2 * half), jnp.bfloat16),
        input_output_aliases={9: 0} if extra else {},
        compiler_params=PARAMS,
        name="grad_head",
    )(scalars, *grads, *[h for hidden in hiddens for h in (hidden, hidden)], *extra)


def in_hbm(value):
    return pltpu.with_memory_space_constraint(value, pltpu.HBM)


def per_device(
    hidden, head_weight, targets, segment_ids, lengths, loss_mask, advantages, ref_logprobs
):
    bf16, f32 = jnp.bfloat16, jnp.float32
    depth, width = head_weight.shape
    nz, ncore = lax.axis_size("z"), lax.axis_size("core")
    nv = lax.axis_size("x") * lax.axis_size("y")
    block = hidden.shape[0]
    rows = block // nv
    dp, z, core = lax.axis_index("dp"), lax.axis_index("z"), lax.axis_index("core")
    place = lax.axis_index(("x", "y"))
    half, piece = depth // 2, depth // 2 // nv

    straight = lax.all_gather(hidden[:, :half], ("dp", "z"), axis=0, tiled=True)
    share = lax.dynamic_slice_in_dim(hidden, half + place * piece, piece, 1)
    share = spread(share, "z").reshape(nz * block, piece)
    pieces = spread(share, ("x", "y"))
    weights = [in_hbm(w) for w in (head_weight.T, swap(head_weight.T, "core"))]
    scalars = jnp.stack(
        [dp, 1 - dp] + [((z * ncore + c) * nv + place) * width for c in (core, 1 - core)]
    )

    seq_onehot = segment_ids[:, None] == lax.iota(jnp.int32, advantages.shape[0])[None, :]
    token_adv = jnp.sum(jnp.where(seq_onehot, advantages[None, :], 0.0), axis=1)
    token_len = jnp.sum(jnp.where(seq_onehot, lengths[None, :].astype(f32), 0.0), axis=1)
    token_weight = LOSS_SCALE * loss_mask.astype(f32) / token_len
    own = jnp.stack([token_adv, token_weight, ref_logprobs, targets.astype(f32)])
    own = own.reshape(4, nz, ncore, block)
    own = jnp.where(core == 0, own[:, :, 0], own[:, :, 1]).reshape(4, nz * block)
    other = swap(own, "dp")
    later, straight, pieces, other = lax.optimization_barrier(
        (hidden[:, half:], straight, pieces, other)
    )
    straight2 = lax.all_gather(later, ("dp", "z"), axis=0, tiled=True)
    own_target, other_target = own[3:4].astype(jnp.int32), other[3:4].astype(jnp.int32)

    *logits, stats = logits_and_stats(
        scalars, own_target, in_hbm(straight), pieces, weights
    )
    stats = jnp.stack(combine(exchange(stats, "z")))
    parts = spread(stats, ("x", "y"))
    logits = [in_hbm(value) for value in logits]
    partial, own0, own1, final = gradient_partial(
        scalars, own_target, own, parts, logits, weights, nz, nv
    )
    got = lax.all_to_all(partial.reshape(nv, nz * rows, depth), ("x", "y"), 0, 0, tiled=True)
    gathered = (in_hbm(straight), in_hbm(straight2))
    other0, other1 = other_gradient(
        scalars, other_target, other, swap(final, "dp"), gathered, weights
    )
    grads = (own0, other0, swap(own1, "core"), swap(other1, "core"))
    grad_head = head_half(scalars, grads, (gathered[0], in_hbm(swap(straight, "core"))))
    got, straight2, grad_head = lax.optimization_barrier((got, straight2, grad_head))
    grad_head = head_half(
        scalars, grads, (gathered[1], in_hbm(swap(straight2, "core"))), grad_head
    )
    got = jnp.sum(got.astype(f32), axis=0).astype(bf16)
    grad_hidden = scatter_sum(got.reshape(nz, rows, depth), "z").astype(bf16)
    return grad_hidden, grad_head.T


def solution(mesh):
    devices = mesh.devices.reshape(2, 4, 2, 4, 4)
    fine = Mesh(devices, ("dp", "z", "core", "x", "y"))
    ctx, vocab = ("z", "core"), ("x", "y")
    return jax.shard_map(
        per_device,
        mesh=fine,
        in_specs=(
            P(("dp",) + ctx, None),
            P(None, ctx + vocab),
            P("dp"),
            P("dp"),
            P(),
            P("dp"),
            P(),
            P("dp"),
        ),
        out_specs=(P(("dp",) + ctx + vocab, None), P(None, ctx + vocab)),
        check_vma=False,
    )
```

```python
import functools

import jax
import jax.numpy as jnp
from jax import lax
from jax.experimental import pallas as pl
from jax.experimental.pallas import tpu as pltpu
from jax.sharding import Mesh, PartitionSpec as P

LOSS_SCALE = 1024
KL_WEIGHT = 0.1
ENTROPY_WEIGHT = 0.05


def combine(parts):
    top = parts[0][0]
    for part in parts[1:]:
        top = jnp.maximum(top, part[0])
    scales = [jnp.exp(part[0] - top) for part in parts]
    total = sum(part[1] * scale for part, scale in zip(parts, scales))
    logit = sum(part[2] * scale for part, scale in zip(parts, scales))
    target = sum(part[3] for part in parts)
    return [top, total, logit, target]


def exchange(stats, axis):
    size = lax.axis_size(axis)
    others = [
        lax.ppermute(stats, axis, [(i, (i + step) % size) for i in range(size)])
        for step in range(1, size)
    ]
    return [stats] + others


def spread(value, axis):
    count = lax.axis_size(axis)
    copies = jnp.broadcast_to(value[None], (count,) + value.shape)
    return lax.all_to_all(copies, axis, 0, 0, tiled=True)


def swap(value, axis):
    return lax.ppermute(value, axis, [(0, 1), (1, 0)])


TILE = 2048
HEAD_TILE = 1024
PARAMS = pltpu.CompilerParams(vmem_limit_bytes=24 * 2**20)


def whole(*shape):
    return pl.BlockSpec(shape, lambda i, s: (0,) * len(shape))


def tiles(rows):
    return pl.BlockSpec((rows, TILE), lambda i, s: (0, i))


def hidden_specs(tokens, depth, group):
    lead = depth // TILE // 2
    return [
        pl.BlockSpec((tokens, TILE), lambda i, s: (s[group], jnp.minimum(i, lead - 1))),
        pl.BlockSpec((tokens, TILE), lambda i, s: (s[group], jnp.maximum(i - lead, 0))),
    ]


def call(kernel, name, depth, in_specs, out_specs, out_shape, scratch=(), flops=0):
    return pl.pallas_call(
        kernel,
        grid_spec=pltpu.PrefetchScalarGridSpec(
            num_scalar_prefetch=1,
            grid=(depth // TILE,),
            in_specs=in_specs,
            out_specs=out_specs,
            scratch_shapes=list(scratch),
        ),
        out_shape=out_shape,
        compiler_params=PARAMS,
        cost_estimate=pl.CostEstimate(flops=flops, bytes_accessed=flops // 500, transcendentals=0),
        name=name,
    )


def halves(use_first, use_second):
    step, lead = pl.program_id(0), pl.num_programs(0) // 2
    pl.when(step < lead)(use_first)
    pl.when(step >= lead)(use_second)


def add_logits(tile, weights, logits):
    for weight, out in zip(weights, logits):
        out[...] += lax.dot_general(
            weight[...], tile, (((1,), (1,)), ((), ())), preferred_element_type=jnp.float32
        )


def hits(value, first, target):
    return first + lax.broadcasted_iota(jnp.int32, value.shape, 0) == target[...]


def logits_kernel(s, target, straight, pieces, weight0, weight1, logits0, logits1, stats):
    step = pl.program_id(0)

    @pl.when(step == 0)
    def _():
        logits0[...] = jnp.zeros_like(logits0)
        logits1[...] = jnp.zeros_like(logits1)

    def use_second():
        tile = jnp.concatenate([pieces[j] for j in range(pieces.shape[0])], axis=1)
        add_logits(tile, (weight0, weight1), (logits0, logits1))

    halves(
        lambda: add_logits(straight[...], (weight0, weight1), (logits0, logits1)), use_second
    )

    @pl.when(step == pl.num_programs(0) - 1)
    def _():
        top = jnp.maximum(
            jnp.max(logits0[...], axis=0, keepdims=True),
            jnp.max(logits1[...], axis=0, keepdims=True),
        )
        stats[0:1, :] = top
        total, weighted, hit_sum = 0.0, 0.0, 0.0
        for k, logits in enumerate((logits0, logits1)):
            value = logits[...]
            shifted = jnp.exp(value - top)
            hit = jnp.where(hits(value, s[2 + k], target), value, 0.0)
            total += jnp.sum(shifted, axis=0, keepdims=True)
            weighted += jnp.sum(shifted * value, axis=0, keepdims=True)
            hit_sum += jnp.sum(hit, axis=0, keepdims=True)
        stats[1:2, :] = total
        stats[2:3, :] = weighted
        stats[3:4, :] = hit_sum


def logits_and_stats(scalars, target, straight, pieces, weights):
    width, depth = weights[0].shape
    tokens, piece = pieces.shape[1:]
    lead = depth // TILE // 2
    return call(
        logits_kernel,
        "logits",
        depth,
        [
            whole(1, tokens),
            hidden_specs(tokens, depth, 0)[0],
            pl.BlockSpec(
                (TILE // piece, tokens, piece), lambda i, s: (jnp.maximum(i - lead, 0), 0, 0)
            ),
            tiles(width),
            tiles(width),
        ],
        [whole(width, tokens)] * 2 + [whole(4, tokens)],
        [pltpu.HBM((width, tokens), jnp.float32)] * 2
        + [jax.ShapeDtypeStruct((4, tokens), jnp.float32)],
        flops=4 * tokens * width * depth,
    )(scalars, target, straight, pieces, *weights)


def logit_gradient(value, first, target, info, final):
    adv, weight, ref_logp = [info[i : i + 1, :] for i in range(3)]
    log_total, target_logp, mean_logit = final
    logp_grad = -adv + KL_WEIGHT * (target_logp - ref_logp)
    hit = jnp.where(hits(value, first, target), 1.0, 0.0)
    probs = jnp.exp(value - log_total)
    inner = logp_grad * (hit - probs)
    inner = inner + ENTROPY_WEIGHT * probs * (value - mean_logit)
    return (weight * inner).astype(jnp.bfloat16)


def gradient_kernel(
    s, target, info, parts, logits0, logits1, weight0, weight1,
    out, grad0, grad1, final, held0, held1, *, nz, nv,
):
    @pl.when(pl.program_id(0) == 0)
    def _():
        count, tokens = parts.shape[0], parts.shape[2]
        row_max, exp_total, exp_logit, target_logit = combine(
            [[parts[j, i : i + 1, :] for i in range(4)] for j in range(count)]
        )
        log_total = row_max + jnp.log(exp_total)
        ends = (log_total, target_logit - log_total, exp_logit / exp_total)
        for i, end in enumerate(ends):
            final[i : i + 1, :] = end
        rows = tokens // (nz * nv)
        row = lax.broadcasted_iota(jnp.int32, (tokens, tokens), 0)
        token = lax.broadcasted_iota(jnp.int32, (tokens, tokens), 1)
        source = (row // rows % nz * nv + row // (rows * nz)) * rows + row % rows
        order = jnp.where(token == source, 1.0, 0.0).astype(jnp.bfloat16)
        sets = ((logits0, grad0, held0), (logits1, grad1, held1))
        for k, (logits, grad, held) in enumerate(sets):
            result = logit_gradient(logits[...], s[2 + k], target, info, ends)
            grad[...] = result
            held[...] = lax.dot_general(
                order, result, (((1,), (1,)), ((), ())), preferred_element_type=jnp.float32
            ).astype(jnp.bfloat16)

    out[...] = (
        jnp.dot(held0[...], weight0[...], preferred_element_type=jnp.float32)
        + jnp.dot(held1[...], weight1[...], preferred_element_type=jnp.float32)
    ).astype(jnp.bfloat16)


def gradient_partial(scalars, target, info, parts, logits, weights, nz, nv):
    width, depth = weights[0].shape
    tokens = info.shape[1]
    return call(
        functools.partial(gradient_kernel, nz=nz, nv=nv),
        "grad_hidden_partial",
        depth,
        [whole(1, tokens), whole(4, tokens), whole(*parts.shape)]
        + [whole(width, tokens)] * 2
        + [tiles(width)] * 2,
        [tiles(tokens)] + [whole(width, tokens)] * 2 + [whole(3, tokens)],
        [pltpu.HBM((tokens, depth), jnp.bfloat16)]
        + [pltpu.HBM((width, tokens), jnp.bfloat16)] * 2
        + [jax.ShapeDtypeStruct((3, tokens), jnp.float32)],
        [pltpu.VMEM((tokens, width), jnp.bfloat16)] * 2,
        flops=4 * tokens * width * depth,
    )(scalars, target, info, parts, *logits, *weights)


def other_kernel(
    s, target, info, final, straight, straight2, weight0, weight1, grad0, grad1, logits0, logits1
):
    step = pl.program_id(0)

    @pl.when(step == 0)
    def _():
        logits0[...] = jnp.zeros_like(logits0)
        logits1[...] = jnp.zeros_like(logits1)

    halves(
        lambda: add_logits(straight[...], (weight0, weight1), (logits0, logits1)),
        lambda: add_logits(straight2[...], (weight0, weight1), (logits0, logits1)),
    )

    @pl.when(step == pl.num_programs(0) - 1)
    def _():
        ends = [final[i : i + 1, :] for i in range(3)]
        for k, (logits, grad) in enumerate(((logits0, grad0), (logits1, grad1))):
            grad[...] = logit_gradient(logits[...], s[2 + k], target, info, ends)


def other_gradient(scalars, target, info, final, straights, weights):
    width, depth = weights[0].shape
    tokens = info.shape[1]
    return call(
        other_kernel,
        "other_group_grad_logits",
        depth,
        [whole(1, tokens), whole(4, tokens), whole(3, tokens)]
        + hidden_specs(tokens, depth, 1)
        + [tiles(width)] * 2,
        [whole(width, tokens)] * 2,
        [pltpu.HBM((width, tokens), jnp.bfloat16)] * 2,
        [pltpu.VMEM((width, tokens), jnp.float32)] * 2,
        flops=4 * tokens * width * depth,
    )(scalars, target, info, final, *straights, *weights)


def head_kernel(s, *refs, count):
    out, total = refs[-1], 0.0
    for grad, hidden in zip(refs[:count], refs[count : 2 * count]):
        total = total + jnp.dot(grad[...], hidden[...], preferred_element_type=jnp.float32)
    out[...] = total.astype(jnp.bfloat16)


def head_half(scalars, grads, hiddens, before=None):
    width, tokens = grads[0].shape
    half = hiddens[0].shape[1]
    steps = half // HEAD_TILE
    skip = 0 if before is None else steps
    extra = [] if before is None else [before]
    rows = [pl.BlockSpec((tokens, HEAD_TILE), lambda i, s, g=g: (s[g], i)) for g in (0, 1)]
    return pl.pallas_call(
        functools.partial(head_kernel, count=4),
        grid_spec=pltpu.PrefetchScalarGridSpec(
            num_scalar_prefetch=1,
            grid=(steps,),
            in_specs=[whole(width, tokens)] * 4
            + rows * 2
            + [pl.BlockSpec(memory_space=pl.ANY)] * len(extra),
            out_specs=pl.BlockSpec((width, HEAD_TILE), lambda i, s: (0, i + skip)),
        ),
        out_shape=pltpu.HBM((width, 2 * half), jnp.bfloat16),
        input_output_aliases={9: 0} if extra else {},
        compiler_params=PARAMS,
        name="grad_head",
    )(scalars, *grads, *[h for hidden in hiddens for h in (hidden, hidden)], *extra)


def in_hbm(value):
    return pltpu.with_memory_space_constraint(value, pltpu.HBM)


def per_device(
    hidden, head_weight, targets, segment_ids, lengths, loss_mask, advantages, ref_logprobs
):
    bf16, f32 = jnp.bfloat16, jnp.float32
    depth, width = head_weight.shape
    nz, ncore = lax.axis_size("z"), lax.axis_size("core")
    nv = lax.axis_size("x") * lax.axis_size("y")
    block = hidden.shape[0]
    rows = block // nv
    dp, z, core = lax.axis_index("dp"), lax.axis_index("z"), lax.axis_index("core")
    place = lax.axis_index(("x", "y"))
    half, piece = depth // 2, depth // 2 // nv

    straight = lax.all_gather(hidden[:, :half], ("dp", "z"), axis=0, tiled=True)
    share = lax.dynamic_slice_in_dim(hidden, half + place * piece, piece, 1)
    share = spread(share, "z").reshape(nz * block, piece)
    pieces = spread(share, ("x", "y"))
    weights = [in_hbm(w) for w in (head_weight.T, swap(head_weight.T, "core"))]
    scalars = jnp.stack(
        [dp, 1 - dp] + [((z * ncore + c) * nv + place) * width for c in (core, 1 - core)]
    )

    seq_onehot = segment_ids[:, None] == lax.iota(jnp.int32, advantages.shape[0])[None, :]
    token_adv = jnp.sum(jnp.where(seq_onehot, advantages[None, :], 0.0), axis=1)
    token_len = jnp.sum(jnp.where(seq_onehot, lengths[None, :].astype(f32), 0.0), axis=1)
    token_weight = LOSS_SCALE * loss_mask.astype(f32) / token_len
    own = jnp.stack([token_adv, token_weight, ref_logprobs, targets.astype(f32)])
    own = own.reshape(4, nz, ncore, block)
    own = jnp.where(core == 0, own[:, :, 0], own[:, :, 1]).reshape(4, nz * block)
    other = swap(own, "dp")
    later, straight, pieces, other = lax.optimization_barrier(
        (hidden[:, half:], straight, pieces, other)
    )
    straight2 = lax.all_gather(later, ("dp", "z"), axis=0, tiled=True)
    own_target, other_target = own[3:4].astype(jnp.int32), other[3:4].astype(jnp.int32)

    *logits, stats = logits_and_stats(
        scalars, own_target, in_hbm(straight), pieces, weights
    )
    stats = jnp.stack(combine(exchange(stats, "z")))
    parts = spread(stats, ("x", "y"))
    logits = [in_hbm(value) for value in logits]
    partial, own0, own1, final = gradient_partial(
        scalars, own_target, own, parts, logits, weights, nz, nv
    )
    got = lax.all_to_all(partial.reshape(nv, nz * rows, depth), ("x", "y"), 0, 0, tiled=True)
    gathered = (in_hbm(straight), in_hbm(straight2))
    other0, other1 = other_gradient(
        scalars, other_target, other, swap(final, "dp"), gathered, weights
    )
    grads = [
        in_hbm(grad) for grad in (own0, other0, swap(own1, "core"), swap(other1, "core"))
    ]
    grad_head = head_half(scalars, grads, (gathered[0], in_hbm(swap(straight, "core"))))
    got, straight2, grad_head = lax.optimization_barrier((got, straight2, grad_head))
    grad_head = head_half(
        scalars, grads, (gathered[1], in_hbm(swap(straight2, "core"))), grad_head
    )
    got = jnp.sum(got.astype(f32), axis=0).astype(bf16)

    def block_for(index):
        return lax.dynamic_slice_in_dim(got, index * rows, rows, 0)

    received = [
        lax.ppermute(
            block_for((z + step) % nz), "z", [(i, (i + step) % nz) for i in range(nz)]
        )
        for step in range(1, nz)
    ]
    received, grad_head = lax.optimization_barrier((received, grad_head))
    grad_hidden = block_for(z).astype(f32)
    for part in received:
        grad_hidden = grad_hidden + part.astype(f32)
    grad_hidden = grad_hidden.astype(bf16)
    return grad_hidden, grad_head.T


def solution(mesh):
    devices = mesh.devices.reshape(2, 4, 2, 4, 4)
    fine = Mesh(devices, ("dp", "z", "core", "x", "y"))
    ctx, vocab = ("z", "core"), ("x", "y")
    return jax.shard_map(
        per_device,
        mesh=fine,
        in_specs=(
            P(("dp",) + ctx, None),
            P(None, ctx + vocab),
            P("dp"),
            P("dp"),
            P(),
            P("dp"),
            P(),
            P("dp"),
        ),
        out_specs=(P(("dp",) + ctx + vocab, None), P(None, ctx + vocab)),
        check_vma=False,
    )
```

```python
import functools

import jax
import jax.numpy as jnp
from jax import lax
from jax.experimental import pallas as pl
from jax.experimental.pallas import tpu as pltpu
from jax.sharding import Mesh, PartitionSpec as P

LOSS_SCALE = 1024
KL_WEIGHT = 0.1
ENTROPY_WEIGHT = 0.05


def combine(parts):
    top = parts[0][0]
    for part in parts[1:]:
        top = jnp.maximum(top, part[0])
    scales = [jnp.exp(part[0] - top) for part in parts]
    total = sum(part[1] * scale for part, scale in zip(parts, scales))
    logit = sum(part[2] * scale for part, scale in zip(parts, scales))
    target = sum(part[3] for part in parts)
    return [top, total, logit, target]


def exchange(stats, axis):
    size = lax.axis_size(axis)
    others = [
        lax.ppermute(stats, axis, [(i, (i + step) % size) for i in range(size)])
        for step in range(1, size)
    ]
    return [stats] + others


def spread(value, axis):
    count = lax.axis_size(axis)
    copies = jnp.broadcast_to(value[None], (count,) + value.shape)
    return lax.all_to_all(copies, axis, 0, 0, tiled=True)


def swap(value, axis):
    return lax.ppermute(value, axis, [(0, 1), (1, 0)])


TILE = 2048
HALF_TILE = 1024
PARAMS = pltpu.CompilerParams(vmem_limit_bytes=24 * 2**20)


def whole(*shape):
    return pl.BlockSpec(shape, lambda i, s: (0,) * len(shape))


def tiles(rows):
    return pl.BlockSpec((rows, TILE), lambda i, s: (0, i))


def hidden_specs(tokens, depth, group):
    lead = depth // TILE // 2
    return [
        pl.BlockSpec((tokens, TILE), lambda i, s: (s[group], jnp.minimum(i, lead - 1))),
        pl.BlockSpec((tokens, TILE), lambda i, s: (s[group], jnp.maximum(i - lead, 0))),
    ]


def call(kernel, name, depth, in_specs, out_specs, out_shape, scratch=(), flops=0):
    return pl.pallas_call(
        kernel,
        grid_spec=pltpu.PrefetchScalarGridSpec(
            num_scalar_prefetch=1,
            grid=(depth // TILE,),
            in_specs=in_specs,
            out_specs=out_specs,
            scratch_shapes=list(scratch),
        ),
        out_shape=out_shape,
        compiler_params=PARAMS,
        cost_estimate=pl.CostEstimate(flops=flops, bytes_accessed=flops // 500, transcendentals=0),
        name=name,
    )


def halves(use_first, use_second):
    step, lead = pl.program_id(0), pl.num_programs(0) // 2
    pl.when(step < lead)(use_first)
    pl.when(step >= lead)(use_second)


def add_logits(tile, weights, logits):
    for weight, out in zip(weights, logits):
        out[...] += lax.dot_general(
            weight[...], tile, (((1,), (1,)), ((), ())), preferred_element_type=jnp.float32
        )


def hits(value, first, target):
    return first + lax.broadcasted_iota(jnp.int32, value.shape, 0) == target[...]


def pieces_kernel(pieces, weight0, weight1, logits0, logits1):
    @pl.when(pl.program_id(0) == 0)
    def _():
        logits0[...] = jnp.zeros_like(logits0)
        logits1[...] = jnp.zeros_like(logits1)

    tile = jnp.concatenate([pieces[j] for j in range(pieces.shape[0])], axis=1)
    add_logits(tile, (weight0, weight1), (logits0, logits1))


def second_half_logits(pieces, weights):
    width, depth = weights[0].shape
    tokens, piece = pieces.shape[1:]
    steps = depth // 2 // HALF_TILE
    return pl.pallas_call(
        pieces_kernel,
        grid=(steps,),
        in_specs=[pl.BlockSpec((HALF_TILE // piece, tokens, piece), lambda i: (i, 0, 0))]
        + [pl.BlockSpec((width, HALF_TILE), lambda i: (0, i + steps))] * 2,
        out_specs=[pl.BlockSpec((width, tokens), lambda i: (0, 0))] * 2,
        out_shape=[pltpu.HBM((width, tokens), jnp.float32)] * 2,
        compiler_params=PARAMS,
        name="logits_second_half",
    )(pieces, *weights)


def logits_kernel(
    s, target, straight, before0, before1, weight0, weight1, logits0, logits1, stats
):
    step = pl.program_id(0)

    @pl.when(step == 0)
    def _():
        logits0[...] = before0[...]
        logits1[...] = before1[...]

    add_logits(straight[...], (weight0, weight1), (logits0, logits1))

    @pl.when(step == pl.num_programs(0) - 1)
    def _():
        top = jnp.maximum(
            jnp.max(logits0[...], axis=0, keepdims=True),
            jnp.max(logits1[...], axis=0, keepdims=True),
        )
        stats[0:1, :] = top
        total, weighted, hit_sum = 0.0, 0.0, 0.0
        for k, logits in enumerate((logits0, logits1)):
            value = logits[...]
            shifted = jnp.exp(value - top)
            hit = jnp.where(hits(value, s[2 + k], target), value, 0.0)
            total += jnp.sum(shifted, axis=0, keepdims=True)
            weighted += jnp.sum(shifted * value, axis=0, keepdims=True)
            hit_sum += jnp.sum(hit, axis=0, keepdims=True)
        stats[1:2, :] = total
        stats[2:3, :] = weighted
        stats[3:4, :] = hit_sum


def logits_and_stats(scalars, target, straight, before, weights):
    width, depth = weights[0].shape
    tokens = before[0].shape[1]
    tile = pl.BlockSpec((width, HALF_TILE), lambda i, s: (0, i))
    return pl.pallas_call(
        logits_kernel,
        grid_spec=pltpu.PrefetchScalarGridSpec(
            num_scalar_prefetch=1,
            grid=(depth // 2 // HALF_TILE,),
            in_specs=[
                whole(1, tokens),
                pl.BlockSpec((tokens, HALF_TILE), lambda i, s: (s[0], i)),
            ]
            + [whole(width, tokens)] * 2
            + [tile] * 2,
            out_specs=[whole(width, tokens)] * 2 + [whole(4, tokens)],
        ),
        out_shape=[pltpu.HBM((width, tokens), jnp.float32)] * 2
        + [jax.ShapeDtypeStruct((4, tokens), jnp.float32)],
        compiler_params=PARAMS,
        name="logits",
    )(scalars, target, straight, *before, *weights)


def logit_gradient(value, first, target, info, final):
    adv, weight, ref_logp = [info[i : i + 1, :] for i in range(3)]
    log_total, target_logp, mean_logit = final
    logp_grad = -adv + KL_WEIGHT * (target_logp - ref_logp)
    hit = jnp.where(hits(value, first, target), 1.0, 0.0)
    probs = jnp.exp(value - log_total)
    inner = logp_grad * (hit - probs)
    inner = inner + ENTROPY_WEIGHT * probs * (value - mean_logit)
    return (weight * inner).astype(jnp.bfloat16)


def gradient_kernel(
    s, target, info, parts, logits0, logits1, weight0, weight1,
    out, grad0, grad1, final, held0, held1, *, nz, nv,
):
    @pl.when(pl.program_id(0) == 0)
    def _():
        count, tokens = parts.shape[0], parts.shape[2]
        row_max, exp_total, exp_logit, target_logit = combine(
            [[parts[j, i : i + 1, :] for i in range(4)] for j in range(count)]
        )
        log_total = row_max + jnp.log(exp_total)
        ends = (log_total, target_logit - log_total, exp_logit / exp_total)
        for i, end in enumerate(ends):
            final[i : i + 1, :] = end
        rows = tokens // (nz * nv)
        row = lax.broadcasted_iota(jnp.int32, (tokens, tokens), 0)
        token = lax.broadcasted_iota(jnp.int32, (tokens, tokens), 1)
        source = (row // rows % nz * nv + row // (rows * nz)) * rows + row % rows
        order = jnp.where(token == source, 1.0, 0.0).astype(jnp.bfloat16)
        sets = ((logits0, grad0, held0), (logits1, grad1, held1))
        for k, (logits, grad, held) in enumerate(sets):
            result = logit_gradient(logits[...], s[2 + k], target, info, ends)
            grad[...] = result
            held[...] = lax.dot_general(
                order, result, (((1,), (1,)), ((), ())), preferred_element_type=jnp.float32
            ).astype(jnp.bfloat16)

    out[...] = (
        jnp.dot(held0[...], weight0[...], preferred_element_type=jnp.float32)
        + jnp.dot(held1[...], weight1[...], preferred_element_type=jnp.float32)
    ).astype(jnp.bfloat16)


def gradient_partial(scalars, target, info, parts, logits, weights, nz, nv):
    width, depth = weights[0].shape
    tokens = info.shape[1]
    return call(
        functools.partial(gradient_kernel, nz=nz, nv=nv),
        "grad_hidden_partial",
        depth,
        [whole(1, tokens), whole(4, tokens), whole(*parts.shape)]
        + [whole(width, tokens)] * 2
        + [tiles(width)] * 2,
        [tiles(tokens)] + [whole(width, tokens)] * 2 + [whole(3, tokens)],
        [pltpu.HBM((tokens, depth), jnp.bfloat16)]
        + [pltpu.HBM((width, tokens), jnp.bfloat16)] * 2
        + [jax.ShapeDtypeStruct((3, tokens), jnp.float32)],
        [pltpu.VMEM((tokens, width), jnp.bfloat16)] * 2,
        flops=4 * tokens * width * depth,
    )(scalars, target, info, parts, *logits, *weights)


def other_kernel(
    s, target, info, final, straight, straight2, weight0, weight1, grad0, grad1, logits0, logits1
):
    step = pl.program_id(0)

    @pl.when(step == 0)
    def _():
        logits0[...] = jnp.zeros_like(logits0)
        logits1[...] = jnp.zeros_like(logits1)

    halves(
        lambda: add_logits(straight[...], (weight0, weight1), (logits0, logits1)),
        lambda: add_logits(straight2[...], (weight0, weight1), (logits0, logits1)),
    )

    @pl.when(step == pl.num_programs(0) - 1)
    def _():
        ends = [final[i : i + 1, :] for i in range(3)]
        for k, (logits, grad) in enumerate(((logits0, grad0), (logits1, grad1))):
            grad[...] = logit_gradient(logits[...], s[2 + k], target, info, ends)


def other_gradient(scalars, target, info, final, straights, weights):
    width, depth = weights[0].shape
    tokens = info.shape[1]
    return call(
        other_kernel,
        "other_group_grad_logits",
        depth,
        [whole(1, tokens), whole(4, tokens), whole(3, tokens)]
        + hidden_specs(tokens, depth, 1)
        + [tiles(width)] * 2,
        [whole(width, tokens)] * 2,
        [pltpu.HBM((width, tokens), jnp.bfloat16)] * 2,
        [pltpu.VMEM((width, tokens), jnp.float32)] * 2,
        flops=4 * tokens * width * depth,
    )(scalars, target, info, final, *straights, *weights)


def head_kernel(s, *refs, count):
    out, total = refs[-1], 0.0
    for grad, hidden in zip(refs[:count], refs[count : 2 * count]):
        total = total + jnp.dot(grad[...], hidden[...], preferred_element_type=jnp.float32)
    out[...] = total.astype(jnp.bfloat16)


def head_half(scalars, grads, hiddens, before=None):
    width, tokens = grads[0].shape
    half = hiddens[0].shape[1]
    steps = half // HALF_TILE
    skip = 0 if before is None else steps
    extra = [] if before is None else [before]
    rows = [pl.BlockSpec((tokens, HALF_TILE), lambda i, s, g=g: (s[g], i)) for g in (0, 1)]
    return pl.pallas_call(
        functools.partial(head_kernel, count=4),
        grid_spec=pltpu.PrefetchScalarGridSpec(
            num_scalar_prefetch=1,
            grid=(steps,),
            in_specs=[whole(width, tokens)] * 4
            + rows * 2
            + [pl.BlockSpec(memory_space=pl.ANY)] * len(extra),
            out_specs=pl.BlockSpec((width, HALF_TILE), lambda i, s: (0, i + skip)),
        ),
        out_shape=pltpu.HBM((width, 2 * half), jnp.bfloat16),
        input_output_aliases={9: 0} if extra else {},
        compiler_params=PARAMS,
        name="grad_head",
    )(scalars, *grads, *[h for hidden in hiddens for h in (hidden, hidden)], *extra)


def in_hbm(value):
    return pltpu.with_memory_space_constraint(value, pltpu.HBM)


def per_device(
    hidden, head_weight, targets, segment_ids, lengths, loss_mask, advantages, ref_logprobs
):
    bf16, f32 = jnp.bfloat16, jnp.float32
    depth, width = head_weight.shape
    nz, ncore = lax.axis_size("z"), lax.axis_size("core")
    nv = lax.axis_size("x") * lax.axis_size("y")
    block = hidden.shape[0]
    rows = block // nv
    dp, z, core = lax.axis_index("dp"), lax.axis_index("z"), lax.axis_index("core")
    place = lax.axis_index(("x", "y"))
    half, piece = depth // 2, depth // 2 // nv

    straight = lax.all_gather(hidden[:, :half], ("dp", "z"), axis=0, tiled=True)
    share = lax.dynamic_slice_in_dim(hidden, half + place * piece, piece, 1)
    share = spread(share, "z").reshape(nz * block, piece)
    pieces = spread(share, ("x", "y"))
    weights = [in_hbm(w) for w in (head_weight.T, swap(head_weight.T, "core"))]
    scalars = jnp.stack(
        [dp, 1 - dp] + [((z * ncore + c) * nv + place) * width for c in (core, 1 - core)]
    )

    seq_onehot = segment_ids[:, None] == lax.iota(jnp.int32, advantages.shape[0])[None, :]
    token_adv = jnp.sum(jnp.where(seq_onehot, advantages[None, :], 0.0), axis=1)
    token_len = jnp.sum(jnp.where(seq_onehot, lengths[None, :].astype(f32), 0.0), axis=1)
    token_weight = LOSS_SCALE * loss_mask.astype(f32) / token_len
    own = jnp.stack([token_adv, token_weight, ref_logprobs, targets.astype(f32)])
    own = own.reshape(4, nz, ncore, block)
    own = jnp.where(core == 0, own[:, :, 0], own[:, :, 1]).reshape(4, nz * block)
    other = swap(own, "dp")
    before = second_half_logits(pieces, weights)
    later, straight, before, other = lax.optimization_barrier(
        (hidden[:, half:], straight, before, other)
    )
    straight2 = lax.all_gather(later, ("dp", "z"), axis=0, tiled=True)
    own_target, other_target = own[3:4].astype(jnp.int32), other[3:4].astype(jnp.int32)

    *logits, stats = logits_and_stats(
        scalars, own_target, in_hbm(straight), [in_hbm(part) for part in before], weights
    )
    stats = jnp.stack(combine(exchange(stats, "z")))
    parts = spread(stats, ("x", "y"))
    logits = [in_hbm(value) for value in logits]
    partial, own0, own1, final = gradient_partial(
        scalars, own_target, own, parts, logits, weights, nz, nv
    )
    got = lax.all_to_all(partial.reshape(nv, nz * rows, depth), ("x", "y"), 0, 0, tiled=True)
    gathered = (in_hbm(straight), in_hbm(straight2))
    other0, other1 = other_gradient(
        scalars, other_target, other, swap(final, "dp"), gathered, weights
    )
    own1, other1 = lax.optimization_barrier((own1, other1))
    grads = [
        in_hbm(grad) for grad in (own0, other0, swap(own1, "core"), swap(other1, "core"))
    ]
    grad_head = head_half(scalars, grads, (gathered[0], in_hbm(swap(straight, "core"))))
    got, straight2, grad_head = lax.optimization_barrier((got, straight2, grad_head))
    grad_head = head_half(
        scalars, grads, (gathered[1], in_hbm(swap(straight2, "core"))), grad_head
    )
    got = jnp.sum(got.astype(f32), axis=0).astype(bf16)

    def block_for(index):
        return lax.dynamic_slice_in_dim(got, index * rows, rows, 0)

    received = [
        lax.ppermute(
            block_for((z + step) % nz), "z", [(i, (i + step) % nz) for i in range(nz)]
        )
        for step in range(1, nz)
    ]
    received, grad_head = lax.optimization_barrier((received, grad_head))
    grad_hidden = block_for(z).astype(f32)
    for part in received:
        grad_hidden = grad_hidden + part.astype(f32)
    grad_hidden = grad_hidden.astype(bf16)
    return grad_hidden, grad_head.T


def solution(mesh):
    devices = mesh.devices.reshape(2, 4, 2, 4, 4)
    fine = Mesh(devices, ("dp", "z", "core", "x", "y"))
    ctx, vocab = ("z", "core"), ("x", "y")
    return jax.shard_map(
        per_device,
        mesh=fine,
        in_specs=(
            P(("dp",) + ctx, None),
            P(None, ctx + vocab),
            P("dp"),
            P("dp"),
            P(),
            P("dp"),
            P(),
            P("dp"),
        ),
        out_specs=(P(("dp",) + ctx + vocab, None), P(None, ctx + vocab)),
        check_vma=False,
    )
```

```python
import functools

import jax
import jax.numpy as jnp
from jax import lax
from jax.experimental import pallas as pl
from jax.experimental.pallas import tpu as pltpu
from jax.sharding import Mesh, PartitionSpec as P

LOSS_SCALE = 1024
KL_WEIGHT = 0.1
ENTROPY_WEIGHT = 0.05


def combine(parts):
    top = parts[0][0]
    for part in parts[1:]:
        top = jnp.maximum(top, part[0])
    scales = [jnp.exp(part[0] - top) for part in parts]
    total = sum(part[1] * scale for part, scale in zip(parts, scales))
    logit = sum(part[2] * scale for part, scale in zip(parts, scales))
    target = sum(part[3] for part in parts)
    return [top, total, logit, target]


def exchange(stats, axis):
    size = lax.axis_size(axis)
    others = [
        lax.ppermute(stats, axis, [(i, (i + step) % size) for i in range(size)])
        for step in range(1, size)
    ]
    return [stats] + others


def spread(value, axis):
    count = lax.axis_size(axis)
    copies = jnp.broadcast_to(value[None], (count,) + value.shape)
    return lax.all_to_all(copies, axis, 0, 0, tiled=True)


def swap(value, axis):
    return lax.ppermute(value, axis, [(0, 1), (1, 0)])


TILE = 2048
HALF_TILE = 1024
PARAMS = pltpu.CompilerParams(vmem_limit_bytes=24 * 2**20)


def whole(*shape):
    return pl.BlockSpec(shape, lambda i, s: (0,) * len(shape))


def tiles(rows):
    return pl.BlockSpec((rows, TILE), lambda i, s: (0, i))


def call(kernel, name, depth, in_specs, out_specs, out_shape, scratch=(), flops=0):
    return pl.pallas_call(
        kernel,
        grid_spec=pltpu.PrefetchScalarGridSpec(
            num_scalar_prefetch=1,
            grid=(depth // TILE,),
            in_specs=in_specs,
            out_specs=out_specs,
            scratch_shapes=list(scratch),
        ),
        out_shape=out_shape,
        compiler_params=PARAMS,
        cost_estimate=pl.CostEstimate(flops=flops, bytes_accessed=flops // 500, transcendentals=0),
        name=name,
    )


def add_logits(tile, weights, logits):
    for weight, out in zip(weights, logits):
        out[...] += lax.dot_general(
            weight[...], tile, (((1,), (1,)), ((), ())), preferred_element_type=jnp.float32
        )


def hits(value, first, target):
    return first + lax.broadcasted_iota(jnp.int32, value.shape, 0) == target[...]


def pieces_kernel(pieces, weight0, weight1, logits0, logits1):
    @pl.when(pl.program_id(0) == 0)
    def _():
        logits0[...] = jnp.zeros_like(logits0)
        logits1[...] = jnp.zeros_like(logits1)

    tile = jnp.concatenate([pieces[j] for j in range(pieces.shape[0])], axis=1)
    add_logits(tile, (weight0, weight1), (logits0, logits1))


def second_half_logits(pieces, weights):
    width, depth = weights[0].shape
    tokens, piece = pieces.shape[1:]
    steps = depth // 2 // HALF_TILE
    return pl.pallas_call(
        pieces_kernel,
        grid=(steps,),
        in_specs=[pl.BlockSpec((HALF_TILE // piece, tokens, piece), lambda i: (i, 0, 0))]
        + [pl.BlockSpec((width, HALF_TILE), lambda i: (0, i + steps))] * 2,
        out_specs=[pl.BlockSpec((width, tokens), lambda i: (0, 0))] * 2,
        out_shape=[pltpu.HBM((width, tokens), jnp.float32)] * 2,
        compiler_params=PARAMS,
        name="logits_second_half",
    )(pieces, *weights)


def logits_kernel(
    s, target, straight, other_straight, before0, before1, weight0, weight1,
    logits0, logits1, other0, other1, stats,
):
    step = pl.program_id(0)

    @pl.when(step == 0)
    def _():
        logits0[...] = before0[...]
        logits1[...] = before1[...]
        other0[...] = jnp.zeros_like(other0)
        other1[...] = jnp.zeros_like(other1)

    add_logits(straight[...], (weight0, weight1), (logits0, logits1))
    add_logits(other_straight[...], (weight0, weight1), (other0, other1))

    @pl.when(step == pl.num_programs(0) - 1)
    def _():
        top = jnp.maximum(
            jnp.max(logits0[...], axis=0, keepdims=True),
            jnp.max(logits1[...], axis=0, keepdims=True),
        )
        stats[0:1, :] = top
        total, weighted, hit_sum = 0.0, 0.0, 0.0
        for k, logits in enumerate((logits0, logits1)):
            value = logits[...]
            shifted = jnp.exp(value - top)
            hit = jnp.where(hits(value, s[2 + k], target), value, 0.0)
            total += jnp.sum(shifted, axis=0, keepdims=True)
            weighted += jnp.sum(shifted * value, axis=0, keepdims=True)
            hit_sum += jnp.sum(hit, axis=0, keepdims=True)
        stats[1:2, :] = total
        stats[2:3, :] = weighted
        stats[3:4, :] = hit_sum


def logits_and_stats(scalars, target, straight, before, weights):
    width, depth = weights[0].shape
    tokens = before[0].shape[1]
    tile = pl.BlockSpec((width, HALF_TILE), lambda i, s: (0, i))
    return pl.pallas_call(
        logits_kernel,
        grid_spec=pltpu.PrefetchScalarGridSpec(
            num_scalar_prefetch=1,
            grid=(depth // 2 // HALF_TILE,),
            in_specs=[
                whole(1, tokens),
                pl.BlockSpec((tokens, HALF_TILE), lambda i, s: (s[0], i)),
                pl.BlockSpec((tokens, HALF_TILE), lambda i, s: (s[1], i)),
            ]
            + [whole(width, tokens)] * 2
            + [tile] * 2,
            out_specs=[whole(width, tokens)] * 4 + [whole(4, tokens)],
        ),
        out_shape=[pltpu.HBM((width, tokens), jnp.float32)] * 4
        + [jax.ShapeDtypeStruct((4, tokens), jnp.float32)],
        compiler_params=PARAMS,
        name="logits",
    )(scalars, target, straight, straight, *before, *weights)


def logit_gradient(value, first, target, info, final):
    adv, weight, ref_logp = [info[i : i + 1, :] for i in range(3)]
    log_total, target_logp, mean_logit = final
    logp_grad = -adv + KL_WEIGHT * (target_logp - ref_logp)
    hit = jnp.where(hits(value, first, target), 1.0, 0.0)
    probs = jnp.exp(value - log_total)
    inner = logp_grad * (hit - probs)
    inner = inner + ENTROPY_WEIGHT * probs * (value - mean_logit)
    return (weight * inner).astype(jnp.bfloat16)


def gradient_kernel(
    s, target, info, parts, logits0, logits1, weight0, weight1,
    out, grad0, grad1, final, held0, held1, *, nz, nv,
):
    @pl.when(pl.program_id(0) == 0)
    def _():
        count, tokens = parts.shape[0], parts.shape[2]
        row_max, exp_total, exp_logit, target_logit = combine(
            [[parts[j, i : i + 1, :] for i in range(4)] for j in range(count)]
        )
        log_total = row_max + jnp.log(exp_total)
        ends = (log_total, target_logit - log_total, exp_logit / exp_total)
        for i, end in enumerate(ends):
            final[i : i + 1, :] = end
        rows = tokens // (nz * nv)
        row = lax.broadcasted_iota(jnp.int32, (tokens, tokens), 0)
        token = lax.broadcasted_iota(jnp.int32, (tokens, tokens), 1)
        source = (row // rows % nz * nv + row // (rows * nz)) * rows + row % rows
        order = jnp.where(token == source, 1.0, 0.0).astype(jnp.bfloat16)
        sets = ((logits0, grad0, held0), (logits1, grad1, held1))
        for k, (logits, grad, held) in enumerate(sets):
            result = logit_gradient(logits[...], s[2 + k], target, info, ends)
            grad[...] = result
            held[...] = lax.dot_general(
                order, result, (((1,), (1,)), ((), ())), preferred_element_type=jnp.float32
            ).astype(jnp.bfloat16)

    out[...] = (
        jnp.dot(held0[...], weight0[...], preferred_element_type=jnp.float32)
        + jnp.dot(held1[...], weight1[...], preferred_element_type=jnp.float32)
    ).astype(jnp.bfloat16)


def gradient_partial(scalars, target, info, parts, logits, weights, nz, nv):
    width, depth = weights[0].shape
    tokens = info.shape[1]
    return call(
        functools.partial(gradient_kernel, nz=nz, nv=nv),
        "grad_hidden_partial",
        depth,
        [whole(1, tokens), whole(4, tokens), whole(*parts.shape)]
        + [whole(width, tokens)] * 2
        + [tiles(width)] * 2,
        [tiles(tokens)] + [whole(width, tokens)] * 2 + [whole(3, tokens)],
        [pltpu.HBM((tokens, depth), jnp.bfloat16)]
        + [pltpu.HBM((width, tokens), jnp.bfloat16)] * 2
        + [jax.ShapeDtypeStruct((3, tokens), jnp.float32)],
        [pltpu.VMEM((tokens, width), jnp.bfloat16)] * 2,
        flops=4 * tokens * width * depth,
    )(scalars, target, info, parts, *logits, *weights)


def other_kernel(
    s, target, info, final, before0, before1, straight2, weight0, weight1,
    grad0, grad1, logits0, logits1,
):
    step = pl.program_id(0)

    @pl.when(step == 0)
    def _():
        logits0[...] = before0[...]
        logits1[...] = before1[...]

    add_logits(straight2[...], (weight0, weight1), (logits0, logits1))

    @pl.when(step == pl.num_programs(0) - 1)
    def _():
        ends = [final[i : i + 1, :] for i in range(3)]
        for k, (logits, grad) in enumerate(((logits0, grad0), (logits1, grad1))):
            grad[...] = logit_gradient(logits[...], s[2 + k], target, info, ends)


def other_gradient(scalars, target, info, final, before, straight2, weights):
    width, depth = weights[0].shape
    tokens = info.shape[1]
    steps = depth // 2 // HALF_TILE
    return pl.pallas_call(
        other_kernel,
        grid_spec=pltpu.PrefetchScalarGridSpec(
            num_scalar_prefetch=1,
            grid=(steps,),
            in_specs=[whole(1, tokens), whole(4, tokens), whole(3, tokens)]
            + [whole(width, tokens)] * 2
            + [pl.BlockSpec((tokens, HALF_TILE), lambda i, s: (s[1], i))]
            + [pl.BlockSpec((width, HALF_TILE), lambda i, s: (0, i + steps))] * 2,
            out_specs=[whole(width, tokens)] * 2,
            scratch_shapes=[pltpu.VMEM((width, tokens), jnp.float32)] * 2,
        ),
        out_shape=[pltpu.HBM((width, tokens), jnp.bfloat16)] * 2,
        compiler_params=PARAMS,
        name="other_group_grad_logits",
    )(scalars, target, info, final, *before, straight2, *weights)


def head_kernel(s, *refs, count):
    out, total = refs[-1], 0.0
    for grad, hidden in zip(refs[:count], refs[count : 2 * count]):
        total = total + jnp.dot(grad[...], hidden[...], preferred_element_type=jnp.float32)
    out[...] = total.astype(jnp.bfloat16)


def head_half(scalars, grads, hiddens, before=None):
    width, tokens = grads[0].shape
    half = hiddens[0].shape[1]
    steps = half // HALF_TILE
    skip = 0 if before is None else steps
    extra = [] if before is None else [before]
    rows = [pl.BlockSpec((tokens, HALF_TILE), lambda i, s, g=g: (s[g], i)) for g in (0, 1)]
    return pl.pallas_call(
        functools.partial(head_kernel, count=4),
        grid_spec=pltpu.PrefetchScalarGridSpec(
            num_scalar_prefetch=1,
            grid=(steps,),
            in_specs=[whole(width, tokens)] * 4
            + rows * 2
            + [pl.BlockSpec(memory_space=pl.ANY)] * len(extra),
            out_specs=pl.BlockSpec((width, HALF_TILE), lambda i, s: (0, i + skip)),
        ),
        out_shape=pltpu.HBM((width, 2 * half), jnp.bfloat16),
        input_output_aliases={9: 0} if extra else {},
        compiler_params=PARAMS,
        name="grad_head",
    )(scalars, *grads, *[h for hidden in hiddens for h in (hidden, hidden)], *extra)


def in_hbm(value):
    return pltpu.with_memory_space_constraint(value, pltpu.HBM)


def per_device(
    hidden, head_weight, targets, segment_ids, lengths, loss_mask, advantages, ref_logprobs
):
    bf16, f32 = jnp.bfloat16, jnp.float32
    depth, width = head_weight.shape
    nz, ncore = lax.axis_size("z"), lax.axis_size("core")
    nv = lax.axis_size("x") * lax.axis_size("y")
    block = hidden.shape[0]
    rows = block // nv
    dp, z, core = lax.axis_index("dp"), lax.axis_index("z"), lax.axis_index("core")
    place = lax.axis_index(("x", "y"))
    half, piece = depth // 2, depth // 2 // nv

    straight = lax.all_gather(hidden[:, :half], ("dp", "z"), axis=0, tiled=True)
    share = lax.dynamic_slice_in_dim(hidden, half + place * piece, piece, 1)
    share = spread(share, "z").reshape(nz * block, piece)
    pieces = spread(share, ("x", "y"))
    weights = [in_hbm(w) for w in (head_weight.T, swap(head_weight.T, "core"))]
    scalars = jnp.stack(
        [dp, 1 - dp] + [((z * ncore + c) * nv + place) * width for c in (core, 1 - core)]
    )

    seq_onehot = segment_ids[:, None] == lax.iota(jnp.int32, advantages.shape[0])[None, :]
    token_adv = jnp.sum(jnp.where(seq_onehot, advantages[None, :], 0.0), axis=1)
    token_len = jnp.sum(jnp.where(seq_onehot, lengths[None, :].astype(f32), 0.0), axis=1)
    token_weight = LOSS_SCALE * loss_mask.astype(f32) / token_len
    own = jnp.stack([token_adv, token_weight, ref_logprobs, targets.astype(f32)])
    own = own.reshape(4, nz, ncore, block)
    own = jnp.where(core == 0, own[:, :, 0], own[:, :, 1]).reshape(4, nz * block)
    other = swap(own, "dp")
    before = second_half_logits(pieces, weights)
    later, straight, before, other = lax.optimization_barrier(
        (hidden[:, half:], straight, before, other)
    )
    straight2 = lax.all_gather(later, ("dp", "z"), axis=0, tiled=True)
    own_target, other_target = own[3:4].astype(jnp.int32), other[3:4].astype(jnp.int32)

    logits0, logits1, *other_before, stats = logits_and_stats(
        scalars, own_target, in_hbm(straight), [in_hbm(part) for part in before], weights
    )
    stats = jnp.stack(combine(exchange(stats, "z")))
    parts = spread(stats, ("x", "y"))
    logits = [in_hbm(value) for value in (logits0, logits1)]
    partial, own0, own1, final = gradient_partial(
        scalars, own_target, own, parts, logits, weights, nz, nv
    )
    got = lax.all_to_all(partial.reshape(nv, nz * rows, depth), ("x", "y"), 0, 0, tiled=True)
    gathered = (in_hbm(straight), in_hbm(straight2))
    other0, other1 = other_gradient(
        scalars,
        other_target,
        other,
        swap(final, "dp"),
        [in_hbm(part) for part in other_before],
        gathered[1],
        weights,
    )
    grads = [
        in_hbm(grad) for grad in (own0, other0, swap(own1, "core"), swap(other1, "core"))
    ]
    grad_head = head_half(scalars, grads, (gathered[0], in_hbm(swap(straight, "core"))))
    got, straight2, grad_head = lax.optimization_barrier((got, straight2, grad_head))
    grad_head = head_half(
        scalars, grads, (gathered[1], in_hbm(swap(straight2, "core"))), grad_head
    )
    got = jnp.sum(got.astype(f32), axis=0).astype(bf16)

    def block_for(index):
        return lax.dynamic_slice_in_dim(got, index * rows, rows, 0)

    received = [
        lax.ppermute(
            block_for((z + step) % nz), "z", [(i, (i + step) % nz) for i in range(nz)]
        )
        for step in range(1, nz)
    ]
    received, grad_head = lax.optimization_barrier((received, grad_head))
    grad_hidden = block_for(z).astype(f32)
    for part in received:
        grad_hidden = grad_hidden + part.astype(f32)
    grad_hidden = grad_hidden.astype(bf16)
    return grad_hidden, grad_head.T


def solution(mesh):
    devices = mesh.devices.reshape(2, 4, 2, 4, 4)
    fine = Mesh(devices, ("dp", "z", "core", "x", "y"))
    ctx, vocab = ("z", "core"), ("x", "y")
    return jax.shard_map(
        per_device,
        mesh=fine,
        in_specs=(
            P(("dp",) + ctx, None),
            P(None, ctx + vocab),
            P("dp"),
            P("dp"),
            P(),
            P("dp"),
            P(),
            P("dp"),
        ),
        out_specs=(P(("dp",) + ctx + vocab, None), P(None, ctx + vocab)),
        check_vma=False,
    )
```

```python
import functools

import jax
import jax.numpy as jnp
from jax import lax
from jax.experimental import pallas as pl
from jax.experimental.pallas import tpu as pltpu
from jax.sharding import Mesh, PartitionSpec as P

LOSS_SCALE = 1024
KL_WEIGHT = 0.1
ENTROPY_WEIGHT = 0.05


def combine(parts):
    top = parts[0][0]
    for part in parts[1:]:
        top = jnp.maximum(top, part[0])
    scales = [jnp.exp(part[0] - top) for part in parts]
    total = sum(part[1] * scale for part, scale in zip(parts, scales))
    logit = sum(part[2] * scale for part, scale in zip(parts, scales))
    target = sum(part[3] for part in parts)
    return [top, total, logit, target]


def exchange(stats, axis):
    size = lax.axis_size(axis)
    others = [
        lax.ppermute(stats, axis, [(i, (i + step) % size) for i in range(size)])
        for step in range(1, size)
    ]
    return [stats] + others


def spread(value, axis):
    count = lax.axis_size(axis)
    copies = jnp.broadcast_to(value[None], (count,) + value.shape)
    return lax.all_to_all(copies, axis, 0, 0, tiled=True)


def swap(value, axis):
    return lax.ppermute(value, axis, [(0, 1), (1, 0)])


TILE = 2048
HALF_TILE = 1024
PARAMS = pltpu.CompilerParams(vmem_limit_bytes=24 * 2**20)


def whole(*shape):
    return pl.BlockSpec(shape, lambda i, s: (0,) * len(shape))


def tiles(rows):
    return pl.BlockSpec((rows, TILE), lambda i, s: (0, i))


def hidden_specs(tokens, depth, group):
    lead = depth // TILE // 2
    return [
        pl.BlockSpec((tokens, TILE), lambda i, s: (s[group], jnp.minimum(i, lead - 1))),
        pl.BlockSpec((tokens, TILE), lambda i, s: (s[group], jnp.maximum(i - lead, 0))),
    ]


def call(kernel, name, depth, in_specs, out_specs, out_shape, scratch=(), flops=0):
    return pl.pallas_call(
        kernel,
        grid_spec=pltpu.PrefetchScalarGridSpec(
            num_scalar_prefetch=1,
            grid=(depth // TILE,),
            in_specs=in_specs,
            out_specs=out_specs,
            scratch_shapes=list(scratch),
        ),
        out_shape=out_shape,
        compiler_params=PARAMS,
        cost_estimate=pl.CostEstimate(flops=flops, bytes_accessed=flops // 500, transcendentals=0),
        name=name,
    )


def halves(use_first, use_second):
    step, lead = pl.program_id(0), pl.num_programs(0) // 2
    pl.when(step < lead)(use_first)
    pl.when(step >= lead)(use_second)


def add_logits(tile, weights, logits):
    for weight, out in zip(weights, logits):
        out[...] += lax.dot_general(
            weight[...], tile, (((1,), (1,)), ((), ())), preferred_element_type=jnp.float32
        )


def hits(value, first, target):
    return first + lax.broadcasted_iota(jnp.int32, value.shape, 0) == target[...]


def pieces_kernel(pieces, weight0, weight1, logits0, logits1):
    @pl.when(pl.program_id(0) == 0)
    def _():
        logits0[...] = jnp.zeros_like(logits0)
        logits1[...] = jnp.zeros_like(logits1)

    tile = jnp.concatenate([pieces[j] for j in range(pieces.shape[0])], axis=1)
    add_logits(tile, (weight0, weight1), (logits0, logits1))


def second_half_logits(pieces, weights):
    width, depth = weights[0].shape
    tokens, piece = pieces.shape[1:]
    steps = depth // 2 // HALF_TILE
    return pl.pallas_call(
        pieces_kernel,
        grid=(steps,),
        in_specs=[pl.BlockSpec((HALF_TILE // piece, tokens, piece), lambda i: (i, 0, 0))]
        + [pl.BlockSpec((width, HALF_TILE), lambda i: (0, i + steps))] * 2,
        out_specs=[pl.BlockSpec((width, tokens), lambda i: (0, 0))] * 2,
        out_shape=[pltpu.HBM((width, tokens), jnp.float32)] * 2,
        compiler_params=PARAMS,
        name="logits_second_half",
    )(pieces, *weights)


def logits_kernel(
    s, target, straight, before0, before1, weight0, weight1, logits0, logits1, stats
):
    step = pl.program_id(0)

    @pl.when(step == 0)
    def _():
        logits0[...] = before0[...]
        logits1[...] = before1[...]

    add_logits(straight[...], (weight0, weight1), (logits0, logits1))

    @pl.when(step == pl.num_programs(0) - 1)
    def _():
        top = jnp.maximum(
            jnp.max(logits0[...], axis=0, keepdims=True),
            jnp.max(logits1[...], axis=0, keepdims=True),
        )
        stats[0:1, :] = top
        total, weighted, hit_sum = 0.0, 0.0, 0.0
        for k, logits in enumerate((logits0, logits1)):
            value = logits[...]
            shifted = jnp.exp(value - top)
            hit = jnp.where(hits(value, s[2 + k], target), value, 0.0)
            total += jnp.sum(shifted, axis=0, keepdims=True)
            weighted += jnp.sum(shifted * value, axis=0, keepdims=True)
            hit_sum += jnp.sum(hit, axis=0, keepdims=True)
        stats[1:2, :] = total
        stats[2:3, :] = weighted
        stats[3:4, :] = hit_sum


def logits_and_stats(scalars, target, straight, before, weights):
    width, depth = weights[0].shape
    tokens = before[0].shape[1]
    tile = pl.BlockSpec((width, HALF_TILE), lambda i, s: (0, i))
    return pl.pallas_call(
        logits_kernel,
        grid_spec=pltpu.PrefetchScalarGridSpec(
            num_scalar_prefetch=1,
            grid=(depth // 2 // HALF_TILE,),
            in_specs=[
                whole(1, tokens),
                pl.BlockSpec((tokens, HALF_TILE), lambda i, s: (s[0], i)),
            ]
            + [whole(width, tokens)] * 2
            + [tile] * 2,
            out_specs=[whole(width, tokens)] * 2 + [whole(4, tokens)],
        ),
        out_shape=[pltpu.HBM((width, tokens), jnp.float32)] * 2
        + [jax.ShapeDtypeStruct((4, tokens), jnp.float32)],
        compiler_params=PARAMS,
        name="logits",
    )(scalars, target, straight, *before, *weights)


def logit_gradient(value, first, target, info, final):
    adv, weight, ref_logp = [info[i : i + 1, :] for i in range(3)]
    log_total, target_logp, mean_logit = final
    logp_grad = -adv + KL_WEIGHT * (target_logp - ref_logp)
    hit = jnp.where(hits(value, first, target), 1.0, 0.0)
    probs = jnp.exp(value - log_total)
    inner = logp_grad * (hit - probs)
    inner = inner + ENTROPY_WEIGHT * probs * (value - mean_logit)
    return (weight * inner).astype(jnp.bfloat16)


def gradient_kernel(
    s, target, info, parts, logits0, logits1, weight0, weight1,
    out, grad0, grad1, final, held0, held1, *, nz, nv,
):
    @pl.when(pl.program_id(0) == 0)
    def _():
        count, tokens = parts.shape[0], parts.shape[2]
        row_max, exp_total, exp_logit, target_logit = combine(
            [[parts[j, i : i + 1, :] for i in range(4)] for j in range(count)]
        )
        log_total = row_max + jnp.log(exp_total)
        ends = (log_total, target_logit - log_total, exp_logit / exp_total)
        for i, end in enumerate(ends):
            final[i : i + 1, :] = end
        rows = tokens // (nz * nv)
        row = lax.broadcasted_iota(jnp.int32, (tokens, tokens), 0)
        token = lax.broadcasted_iota(jnp.int32, (tokens, tokens), 1)
        source = (row // rows % nz * nv + row // (rows * nz)) * rows + row % rows
        order = jnp.where(token == source, 1.0, 0.0).astype(jnp.bfloat16)
        sets = ((logits0, grad0, held0), (logits1, grad1, held1))
        for k, (logits, grad, held) in enumerate(sets):
            result = logit_gradient(logits[...], s[2 + k], target, info, ends)
            grad[...] = result
            held[...] = lax.dot_general(
                order, result, (((1,), (1,)), ((), ())), preferred_element_type=jnp.float32
            ).astype(jnp.bfloat16)

    out[...] = (
        jnp.dot(held0[...], weight0[...], preferred_element_type=jnp.float32)
        + jnp.dot(held1[...], weight1[...], preferred_element_type=jnp.float32)
    ).astype(jnp.bfloat16)


def gradient_partial(scalars, target, info, parts, logits, weights, nz, nv):
    width, depth = weights[0].shape
    tokens = info.shape[1]
    return call(
        functools.partial(gradient_kernel, nz=nz, nv=nv),
        "grad_hidden_partial",
        depth,
        [whole(1, tokens), whole(4, tokens), whole(*parts.shape)]
        + [whole(width, tokens)] * 2
        + [tiles(width)] * 2,
        [tiles(tokens)] + [whole(width, tokens)] * 2 + [whole(3, tokens)],
        [pltpu.HBM((tokens, depth), jnp.bfloat16)]
        + [pltpu.HBM((width, tokens), jnp.bfloat16)] * 2
        + [jax.ShapeDtypeStruct((3, tokens), jnp.float32)],
        [pltpu.VMEM((tokens, width), jnp.bfloat16)] * 2,
        flops=4 * tokens * width * depth,
    )(scalars, target, info, parts, *logits, *weights)


def other_kernel(s, straight, straight2, weight0, weight1, logits0, logits1):
    @pl.when(pl.program_id(0) == 0)
    def _():
        logits0[...] = jnp.zeros_like(logits0)
        logits1[...] = jnp.zeros_like(logits1)

    halves(
        lambda: add_logits(straight[...], (weight0, weight1), (logits0, logits1)),
        lambda: add_logits(straight2[...], (weight0, weight1), (logits0, logits1)),
    )


def other_gradient_kernel(first, target, info, final, logits0, logits1, grad0, grad1):
    ends = [final[i : i + 1, :] for i in range(3)]
    for k, (logits, grad) in enumerate(((logits0, grad0), (logits1, grad1))):
        grad[...] = logit_gradient(logits[...], first[2 + k], target, info, ends)


def other_logits(scalars, tokens, straights, weights):
    width, depth = weights[0].shape
    return call(
        other_kernel,
        "other_group_logits",
        depth,
        hidden_specs(tokens, depth, 1) + [tiles(width)] * 2,
        [whole(width, tokens)] * 2,
        [pltpu.HBM((width, tokens), jnp.float32)] * 2,
    )(scalars, *straights, *weights)


def other_gradient(scalars, target, info, final, logits):
    width, tokens = logits[0].shape
    return pl.pallas_call(
        other_gradient_kernel,
        in_specs=[pl.BlockSpec(memory_space=pltpu.SMEM)]
        + [pl.BlockSpec(memory_space=pltpu.VMEM)] * 5,
        out_specs=[pl.BlockSpec(memory_space=pltpu.VMEM)] * 2,
        out_shape=[pltpu.HBM((width, tokens), jnp.bfloat16)] * 2,
        compiler_params=PARAMS,
        name="other_group_grad_logits",
    )(scalars, target, info, final, *logits)


def head_kernel(s, *refs, count):
    out, total = refs[-1], 0.0
    for grad, hidden in zip(refs[:count], refs[count : 2 * count]):
        total = total + jnp.dot(grad[...], hidden[...], preferred_element_type=jnp.float32)
    out[...] = total.astype(jnp.bfloat16)


def head_half(scalars, grads, hiddens, before=None):
    width, tokens = grads[0].shape
    half = hiddens[0].shape[1]
    steps = half // HALF_TILE
    skip = 0 if before is None else steps
    extra = [] if before is None else [before]
    rows = [pl.BlockSpec((tokens, HALF_TILE), lambda i, s, g=g: (s[g], i)) for g in (0, 1)]
    return pl.pallas_call(
        functools.partial(head_kernel, count=4),
        grid_spec=pltpu.PrefetchScalarGridSpec(
            num_scalar_prefetch=1,
            grid=(steps,),
            in_specs=[whole(width, tokens)] * 4
            + rows * 2
            + [pl.BlockSpec(memory_space=pl.ANY)] * len(extra),
            out_specs=pl.BlockSpec((width, HALF_TILE), lambda i, s: (0, i + skip)),
        ),
        out_shape=pltpu.HBM((width, 2 * half), jnp.bfloat16),
        input_output_aliases={9: 0} if extra else {},
        compiler_params=PARAMS,
        name="grad_head",
    )(scalars, *grads, *[h for hidden in hiddens for h in (hidden, hidden)], *extra)


def in_hbm(value):
    return pltpu.with_memory_space_constraint(value, pltpu.HBM)


def per_device(
    hidden, head_weight, targets, segment_ids, lengths, loss_mask, advantages, ref_logprobs
):
    bf16, f32 = jnp.bfloat16, jnp.float32
    depth, width = head_weight.shape
    nz, ncore = lax.axis_size("z"), lax.axis_size("core")
    nv = lax.axis_size("x") * lax.axis_size("y")
    block = hidden.shape[0]
    rows = block // nv
    dp, z, core = lax.axis_index("dp"), lax.axis_index("z"), lax.axis_index("core")
    place = lax.axis_index(("x", "y"))
    half, piece = depth // 2, depth // 2 // nv

    straight = lax.all_gather(hidden[:, :half], ("dp", "z"), axis=0, tiled=True)
    share = lax.dynamic_slice_in_dim(hidden, half + place * piece, piece, 1)
    share = spread(share, "z").reshape(nz * block, piece)
    pieces = spread(share, ("x", "y"))
    weights = [in_hbm(w) for w in (head_weight.T, swap(head_weight.T, "core"))]
    scalars = jnp.stack(
        [dp, 1 - dp] + [((z * ncore + c) * nv + place) * width for c in (core, 1 - core)]
    )

    seq_onehot = segment_ids[:, None] == lax.iota(jnp.int32, advantages.shape[0])[None, :]
    token_adv = jnp.sum(jnp.where(seq_onehot, advantages[None, :], 0.0), axis=1)
    token_len = jnp.sum(jnp.where(seq_onehot, lengths[None, :].astype(f32), 0.0), axis=1)
    token_weight = LOSS_SCALE * loss_mask.astype(f32) / token_len
    own = jnp.stack([token_adv, token_weight, ref_logprobs, targets.astype(f32)])
    own = own.reshape(4, nz, ncore, block)
    own = jnp.where(core == 0, own[:, :, 0], own[:, :, 1]).reshape(4, nz * block)
    other = swap(own, "dp")
    before = second_half_logits(pieces, weights)
    later, straight, before, other = lax.optimization_barrier(
        (hidden[:, half:], straight, before, other)
    )
    straight2 = lax.all_gather(later, ("dp", "z"), axis=0, tiled=True)
    own_target, other_target = own[3:4].astype(jnp.int32), other[3:4].astype(jnp.int32)

    *logits, stats = logits_and_stats(
        scalars, own_target, in_hbm(straight), [in_hbm(part) for part in before], weights
    )
    stats = jnp.stack(combine(exchange(stats, "z")))
    parts = spread(stats, ("x", "y"))
    logits = [in_hbm(value) for value in logits]
    partial, own0, own1, final = gradient_partial(
        scalars, own_target, own, parts, logits, weights, nz, nv
    )
    got = lax.all_to_all(partial.reshape(nv, nz * rows, depth), ("x", "y"), 0, 0, tiled=True)
    moved = swap(final, "dp")
    straight2, own1 = lax.optimization_barrier((straight2, own1))
    gathered = (in_hbm(straight), in_hbm(straight2))
    logits = other_logits(scalars, nz * block, gathered, weights)
    moved, logits = lax.optimization_barrier((moved, logits))
    other0, other1 = other_gradient(scalars, other_target, other, moved, logits)
    grads = [
        in_hbm(grad) for grad in (own0, other0, swap(own1, "core"), swap(other1, "core"))
    ]
    grad_head = head_half(scalars, grads, (gathered[0], in_hbm(swap(straight, "core"))))
    got, straight2, grad_head = lax.optimization_barrier((got, straight2, grad_head))
    grad_head = head_half(
        scalars, grads, (gathered[1], in_hbm(swap(straight2, "core"))), grad_head
    )
    got = jnp.sum(got.astype(f32), axis=0).astype(bf16)

    def block_for(index):
        return lax.dynamic_slice_in_dim(got, index * rows, rows, 0)

    received = [
        lax.ppermute(
            block_for((z + step) % nz), "z", [(i, (i + step) % nz) for i in range(nz)]
        )
        for step in range(1, nz)
    ]
    received, grad_head = lax.optimization_barrier((received, grad_head))
    grad_hidden = block_for(z).astype(f32)
    for part in received:
        grad_hidden = grad_hidden + part.astype(f32)
    grad_hidden = grad_hidden.astype(bf16)
    return grad_hidden, grad_head.T


def solution(mesh):
    devices = mesh.devices.reshape(2, 4, 2, 4, 4)
    fine = Mesh(devices, ("dp", "z", "core", "x", "y"))
    ctx, vocab = ("z", "core"), ("x", "y")
    return jax.shard_map(
        per_device,
        mesh=fine,
        in_specs=(
            P(("dp",) + ctx, None),
            P(None, ctx + vocab),
            P("dp"),
            P("dp"),
            P(),
            P("dp"),
            P(),
            P("dp"),
        ),
        out_specs=(P(("dp",) + ctx + vocab, None), P(None, ctx + vocab)),
        check_vma=False,
    )
```

```python
import functools

import jax
import jax.numpy as jnp
from jax import lax
from jax.experimental import pallas as pl
from jax.experimental.pallas import tpu as pltpu
from jax.sharding import Mesh, PartitionSpec as P

LOSS_SCALE = 1024
KL_WEIGHT = 0.1
ENTROPY_WEIGHT = 0.05


def combine(parts):
    top = parts[0][0]
    for part in parts[1:]:
        top = jnp.maximum(top, part[0])
    scales = [jnp.exp(part[0] - top) for part in parts]
    total = sum(part[1] * scale for part, scale in zip(parts, scales))
    logit = sum(part[2] * scale for part, scale in zip(parts, scales))
    target = sum(part[3] for part in parts)
    return [top, total, logit, target]


def exchange(stats, axis):
    size = lax.axis_size(axis)
    others = [
        lax.ppermute(stats, axis, [(i, (i + step) % size) for i in range(size)])
        for step in range(1, size)
    ]
    return [stats] + others


def spread(value, axis):
    count = lax.axis_size(axis)
    copies = jnp.broadcast_to(value[None], (count,) + value.shape)
    return lax.all_to_all(copies, axis, 0, 0, tiled=True)


def swap(value, axis):
    return lax.ppermute(value, axis, [(0, 1), (1, 0)])


TILE = 2048
HALF_TILE = 1024
PARAMS = pltpu.CompilerParams(vmem_limit_bytes=24 * 2**20)


def whole(*shape):
    return pl.BlockSpec(shape, lambda i, s: (0,) * len(shape))


def tiles(rows):
    return pl.BlockSpec((rows, TILE), lambda i, s: (0, i))


def hidden_specs(tokens, depth, group):
    lead = depth // TILE // 2
    return [
        pl.BlockSpec((tokens, TILE), lambda i, s: (s[group], jnp.minimum(i, lead - 1))),
        pl.BlockSpec((tokens, TILE), lambda i, s: (s[group], jnp.maximum(i - lead, 0))),
    ]


def call(kernel, name, depth, in_specs, out_specs, out_shape, scratch=(), flops=0):
    return pl.pallas_call(
        kernel,
        grid_spec=pltpu.PrefetchScalarGridSpec(
            num_scalar_prefetch=1,
            grid=(depth // TILE,),
            in_specs=in_specs,
            out_specs=out_specs,
            scratch_shapes=list(scratch),
        ),
        out_shape=out_shape,
        compiler_params=PARAMS,
        cost_estimate=pl.CostEstimate(flops=flops, bytes_accessed=flops // 500, transcendentals=0),
        name=name,
    )


def halves(use_first, use_second):
    step, lead = pl.program_id(0), pl.num_programs(0) // 2
    pl.when(step < lead)(use_first)
    pl.when(step >= lead)(use_second)


def add_logits(tile, weights, logits):
    for weight, out in zip(weights, logits):
        out[...] += lax.dot_general(
            weight[...], tile, (((1,), (1,)), ((), ())), preferred_element_type=jnp.float32
        )


def hits(value, first, target):
    return first + lax.broadcasted_iota(jnp.int32, value.shape, 0) == target[...]


def pieces_kernel(pieces, weight0, weight1, logits0, logits1):
    @pl.when(pl.program_id(0) == 0)
    def _():
        logits0[...] = jnp.zeros_like(logits0)
        logits1[...] = jnp.zeros_like(logits1)

    tile = jnp.concatenate([pieces[j] for j in range(pieces.shape[0])], axis=1)
    add_logits(tile, (weight0, weight1), (logits0, logits1))


def second_half_logits(pieces, weights):
    width, depth = weights[0].shape
    tokens, piece = pieces.shape[1:]
    steps = depth // 2 // HALF_TILE
    return pl.pallas_call(
        pieces_kernel,
        grid=(steps,),
        in_specs=[pl.BlockSpec((HALF_TILE // piece, tokens, piece), lambda i: (i, 0, 0))]
        + [pl.BlockSpec((width, HALF_TILE), lambda i: (0, i + steps))] * 2,
        out_specs=[pl.BlockSpec((width, tokens), lambda i: (0, 0))] * 2,
        out_shape=[pltpu.HBM((width, tokens), jnp.float32)] * 2,
        compiler_params=PARAMS,
        name="logits_second_half",
    )(pieces, *weights)


def logits_kernel(
    s, target, straight, before0, before1, weight0, weight1, logits0, logits1, stats
):
    step = pl.program_id(0)

    @pl.when(step == 0)
    def _():
        logits0[...] = before0[...]
        logits1[...] = before1[...]

    add_logits(straight[...], (weight0, weight1), (logits0, logits1))

    @pl.when(step == pl.num_programs(0) - 1)
    def _():
        top = jnp.maximum(
            jnp.max(logits0[...], axis=0, keepdims=True),
            jnp.max(logits1[...], axis=0, keepdims=True),
        )
        stats[0:1, :] = top
        total, weighted, hit_sum = 0.0, 0.0, 0.0
        for k, logits in enumerate((logits0, logits1)):
            value = logits[...]
            shifted = jnp.exp(value - top)
            hit = jnp.where(hits(value, s[2 + k], target), value, 0.0)
            total += jnp.sum(shifted, axis=0, keepdims=True)
            weighted += jnp.sum(shifted * value, axis=0, keepdims=True)
            hit_sum += jnp.sum(hit, axis=0, keepdims=True)
        stats[1:2, :] = total
        stats[2:3, :] = weighted
        stats[3:4, :] = hit_sum


def logits_and_stats(scalars, target, straight, before, weights):
    width, depth = weights[0].shape
    tokens = before[0].shape[1]
    tile = pl.BlockSpec((width, HALF_TILE), lambda i, s: (0, i))
    return pl.pallas_call(
        logits_kernel,
        grid_spec=pltpu.PrefetchScalarGridSpec(
            num_scalar_prefetch=1,
            grid=(depth // 2 // HALF_TILE,),
            in_specs=[
                whole(1, tokens),
                pl.BlockSpec((tokens, HALF_TILE), lambda i, s: (s[0], i)),
            ]
            + [whole(width, tokens)] * 2
            + [tile] * 2,
            out_specs=[whole(width, tokens)] * 2 + [whole(4, tokens)],
        ),
        out_shape=[pltpu.HBM((width, tokens), jnp.float32)] * 2
        + [jax.ShapeDtypeStruct((4, tokens), jnp.float32)],
        compiler_params=PARAMS,
        name="logits",
    )(scalars, target, straight, *before, *weights)


def logit_gradient(value, first, target, info, final):
    adv, weight, ref_logp = [info[i : i + 1, :] for i in range(3)]
    log_total, target_logp, mean_logit = final
    logp_grad = -adv + KL_WEIGHT * (target_logp - ref_logp)
    hit = jnp.where(hits(value, first, target), 1.0, 0.0)
    probs = jnp.exp(value - log_total)
    inner = logp_grad * (hit - probs)
    inner = inner + ENTROPY_WEIGHT * probs * (value - mean_logit)
    return (weight * inner).astype(jnp.bfloat16)


def gradient_kernel(
    s, target, info, parts, logits0, logits1, weight0, weight1,
    out, grad0, grad1, final, held0, held1, *, nz, nv,
):
    @pl.when(pl.program_id(0) == 0)
    def _():
        count, tokens = parts.shape[0], parts.shape[2]
        row_max, exp_total, exp_logit, target_logit = combine(
            [[parts[j, i : i + 1, :] for i in range(4)] for j in range(count)]
        )
        log_total = row_max + jnp.log(exp_total)
        ends = (log_total, target_logit - log_total, exp_logit / exp_total)
        for i, end in enumerate(ends):
            final[i : i + 1, :] = end
        rows = tokens // (nz * nv)
        row = lax.broadcasted_iota(jnp.int32, (tokens, tokens), 0)
        token = lax.broadcasted_iota(jnp.int32, (tokens, tokens), 1)
        source = (row // rows % nz * nv + row // (rows * nz)) * rows + row % rows
        order = jnp.where(token == source, 1.0, 0.0).astype(jnp.bfloat16)
        sets = ((logits0, grad0, held0), (logits1, grad1, held1))
        for k, (logits, grad, held) in enumerate(sets):
            result = logit_gradient(logits[...], s[2 + k], target, info, ends)
            grad[...] = result
            held[...] = lax.dot_general(
                order, result, (((1,), (1,)), ((), ())), preferred_element_type=jnp.float32
            ).astype(jnp.bfloat16)

    out[...] = (
        jnp.dot(held0[...], weight0[...], preferred_element_type=jnp.float32)
        + jnp.dot(held1[...], weight1[...], preferred_element_type=jnp.float32)
    ).astype(jnp.bfloat16)


def gradient_partial(scalars, target, info, parts, logits, weights, nz, nv):
    width, depth = weights[0].shape
    tokens = info.shape[1]
    return call(
        functools.partial(gradient_kernel, nz=nz, nv=nv),
        "grad_hidden_partial",
        depth,
        [whole(1, tokens), whole(4, tokens), whole(*parts.shape)]
        + [whole(width, tokens)] * 2
        + [tiles(width)] * 2,
        [tiles(tokens)] + [whole(width, tokens)] * 2 + [whole(3, tokens)],
        [pltpu.HBM((tokens, depth), jnp.bfloat16)]
        + [pltpu.HBM((width, tokens), jnp.bfloat16)] * 2
        + [jax.ShapeDtypeStruct((3, tokens), jnp.float32)],
        [pltpu.VMEM((tokens, width), jnp.bfloat16)] * 2,
        flops=4 * tokens * width * depth,
    )(scalars, target, info, parts, *logits, *weights)


def other_kernel(s, straight, straight2, weight0, weight1, logits0, logits1):
    @pl.when(pl.program_id(0) == 0)
    def _():
        logits0[...] = jnp.zeros_like(logits0)
        logits1[...] = jnp.zeros_like(logits1)

    halves(
        lambda: add_logits(straight[...], (weight0, weight1), (logits0, logits1)),
        lambda: add_logits(straight2[...], (weight0, weight1), (logits0, logits1)),
    )


def other_gradient_kernel(first, target, info, final, logits0, logits1, grad0, grad1):
    ends = [final[i : i + 1, :] for i in range(3)]
    for k, (logits, grad) in enumerate(((logits0, grad0), (logits1, grad1))):
        grad[...] = logit_gradient(logits[...], first[2 + k], target, info, ends)


def other_logits(scalars, tokens, straights, weights):
    width, depth = weights[0].shape
    return call(
        other_kernel,
        "other_group_logits",
        depth,
        hidden_specs(tokens, depth, 1) + [tiles(width)] * 2,
        [whole(width, tokens)] * 2,
        [jax.ShapeDtypeStruct((width, tokens), jnp.float32)] * 2,
    )(scalars, *straights, *weights)


def other_gradient(scalars, target, info, final, logits):
    width, tokens = logits[0].shape
    return pl.pallas_call(
        other_gradient_kernel,
        in_specs=[pl.BlockSpec(memory_space=pltpu.SMEM)]
        + [pl.BlockSpec(memory_space=pltpu.VMEM)] * 5,
        out_specs=[pl.BlockSpec(memory_space=pltpu.VMEM)] * 2,
        out_shape=[pltpu.HBM((width, tokens), jnp.bfloat16)] * 2,
        compiler_params=PARAMS,
        name="other_group_grad_logits",
    )(scalars, target, info, final, *logits)


def head_kernel(s, *refs, count):
    out, total = refs[-1], 0.0
    for grad, hidden in zip(refs[:count], refs[count : 2 * count]):
        total = total + jnp.dot(grad[...], hidden[...], preferred_element_type=jnp.float32)
    out[...] = total.astype(jnp.bfloat16)


def head_half(scalars, grads, hiddens, before=None):
    width, tokens = grads[0].shape
    half = hiddens[0].shape[1]
    steps = half // HALF_TILE
    skip = 0 if before is None else steps
    extra = [] if before is None else [before]
    rows = [pl.BlockSpec((tokens, HALF_TILE), lambda i, s, g=g: (s[g], i)) for g in (0, 1)]
    return pl.pallas_call(
        functools.partial(head_kernel, count=4),
        grid_spec=pltpu.PrefetchScalarGridSpec(
            num_scalar_prefetch=1,
            grid=(steps,),
            in_specs=[whole(width, tokens)] * 4
            + rows * 2
            + [pl.BlockSpec(memory_space=pl.ANY)] * len(extra),
            out_specs=pl.BlockSpec((width, HALF_TILE), lambda i, s: (0, i + skip)),
        ),
        out_shape=pltpu.HBM((width, 2 * half), jnp.bfloat16),
        input_output_aliases={9: 0} if extra else {},
        compiler_params=PARAMS,
        name="grad_head",
    )(scalars, *grads, *[h for hidden in hiddens for h in (hidden, hidden)], *extra)


def in_hbm(value):
    return pltpu.with_memory_space_constraint(value, pltpu.HBM)


def per_device(
    hidden, head_weight, targets, segment_ids, lengths, loss_mask, advantages, ref_logprobs
):
    bf16, f32 = jnp.bfloat16, jnp.float32
    depth, width = head_weight.shape
    nz, ncore = lax.axis_size("z"), lax.axis_size("core")
    nv = lax.axis_size("x") * lax.axis_size("y")
    block = hidden.shape[0]
    rows = block // nv
    dp, z, core = lax.axis_index("dp"), lax.axis_index("z"), lax.axis_index("core")
    place = lax.axis_index(("x", "y"))
    half, piece = depth // 2, depth // 2 // nv

    straight = lax.all_gather(hidden[:, :half], ("dp", "z"), axis=0, tiled=True)
    share = lax.dynamic_slice_in_dim(hidden, half + place * piece, piece, 1)
    share = spread(share, "z").reshape(nz * block, piece)
    pieces = spread(share, ("x", "y"))
    weights = [in_hbm(w) for w in (head_weight.T, swap(head_weight.T, "core"))]
    scalars = jnp.stack(
        [dp, 1 - dp] + [((z * ncore + c) * nv + place) * width for c in (core, 1 - core)]
    )

    seq_onehot = segment_ids[:, None] == lax.iota(jnp.int32, advantages.shape[0])[None, :]
    token_adv = jnp.sum(jnp.where(seq_onehot, advantages[None, :], 0.0), axis=1)
    token_len = jnp.sum(jnp.where(seq_onehot, lengths[None, :].astype(f32), 0.0), axis=1)
    token_weight = LOSS_SCALE * loss_mask.astype(f32) / token_len
    own = jnp.stack([token_adv, token_weight, ref_logprobs, targets.astype(f32)])
    own = own.reshape(4, nz, ncore, block)
    own = jnp.where(core == 0, own[:, :, 0], own[:, :, 1]).reshape(4, nz * block)
    other = swap(own, "dp")
    before = second_half_logits(pieces, weights)
    later, straight, before, other = lax.optimization_barrier(
        (hidden[:, half:], straight, before, other)
    )
    straight2 = lax.all_gather(later, ("dp", "z"), axis=0, tiled=True)
    own_target, other_target = own[3:4].astype(jnp.int32), other[3:4].astype(jnp.int32)

    *logits, stats = logits_and_stats(
        scalars, own_target, in_hbm(straight), [in_hbm(part) for part in before], weights
    )
    stats = jnp.stack(combine(exchange(stats, "z")))
    parts = spread(stats, ("x", "y"))
    logits = [in_hbm(value) for value in logits]
    partial, own0, own1, final = gradient_partial(
        scalars, own_target, own, parts, logits, weights, nz, nv
    )
    got = lax.all_to_all(partial.reshape(nv, nz * rows, depth), ("x", "y"), 0, 0, tiled=True)
    moved = swap(final, "dp")
    straight2, own1 = lax.optimization_barrier((straight2, own1))
    gathered = (in_hbm(straight), in_hbm(straight2))
    logits = other_logits(scalars, nz * block, gathered, weights)
    moved, logits = lax.optimization_barrier((moved, logits))
    other0, other1 = other_gradient(scalars, other_target, other, moved, logits)
    grads = [
        in_hbm(grad) for grad in (own0, other0, swap(own1, "core"), swap(other1, "core"))
    ]
    grad_head = head_half(scalars, grads, (gathered[0], in_hbm(swap(straight, "core"))))
    got, straight2, grad_head = lax.optimization_barrier((got, straight2, grad_head))
    grad_head = head_half(
        scalars, grads, (gathered[1], in_hbm(swap(straight2, "core"))), grad_head
    )
    got = jnp.sum(got.astype(f32), axis=0).astype(bf16)

    def block_for(index):
        return lax.dynamic_slice_in_dim(got, index * rows, rows, 0)

    received = [
        lax.ppermute(
            block_for((z + step) % nz), "z", [(i, (i + step) % nz) for i in range(nz)]
        )
        for step in range(1, nz)
    ]
    received, grad_head = lax.optimization_barrier((received, grad_head))
    grad_hidden = block_for(z).astype(f32)
    for part in received:
        grad_hidden = grad_hidden + part.astype(f32)
    grad_hidden = grad_hidden.astype(bf16)
    return grad_hidden, grad_head.T


def solution(mesh):
    devices = mesh.devices.reshape(2, 4, 2, 4, 4)
    fine = Mesh(devices, ("dp", "z", "core", "x", "y"))
    ctx, vocab = ("z", "core"), ("x", "y")
    return jax.shard_map(
        per_device,
        mesh=fine,
        in_specs=(
            P(("dp",) + ctx, None),
            P(None, ctx + vocab),
            P("dp"),
            P("dp"),
            P(),
            P("dp"),
            P(),
            P("dp"),
        ),
        out_specs=(P(("dp",) + ctx + vocab, None), P(None, ctx + vocab)),
        check_vma=False,
    )
```
